256 devices in a mesh: blk: 64 (over x_lo, z, y), rep: 4 (over x_hi, core).
Axes of the slice: x: 4 (x_hi: 2, x_lo: 2; x = x_hi * 2 + x_lo), y: 4, z: 8, core: 2. Of those that a mesh axis runs over, the one named last changes fastest.
Arguments:
- features: bfloat16 [16384, 768], P(('blk', 'rep')), may hold values from -6 to 6
- start_block: float32 [16384, 128], P(('blk', 'rep')), may hold values from -6 to 6
Outputs:
- spectral_rows: float32 [16384, 128], P(('blk', 'rep'))
The draws below stay inside these ranges and needn't reach their ends.
All inputs are finite; a program needn't handle non-finite values.
Results may differ from the reference program's by a relative error of at most 0.0021.
The reference program's roundings to bfloat16 on the way count: a program that leaves them out, or rounds other values in their place, can miss the bound.
Values may be sent and summed in bfloat16 or wider, within the bound.
A program may use at most 64 MiB of HBM per device.

```python
import math
import jax
import jax.numpy as jnp
from jax import lax

D = 768
KV = 128
ITERS = 2
CLIPS = 16384


def steps_of(own_key, dims, pieces, smallest, top_value):
    def one(dim, blocks):
        heights = jax.random.uniform(jax.random.fold_in(jax.random.fold_in(own_key, 6), dim), (blocks,), jnp.float32, smallest / len(pieces), top_value / len(pieces))
        return jnp.repeat(jnp.exp(heights), dims[dim] // blocks).reshape((-1,) + (1,) * (len(dims) - dim - 1))

    gain = one(*pieces[0])
    for cut in pieces[1:]:
        gain = gain * one(*cut)
    return gain


def scatter_about(key, extent, scale, limit, cuts=(), held_as=jnp.bfloat16):
    loudness = steps_of(key, extent, cuts, -0.22, 0.18) if cuts else 1.0
    entries = jax.random.normal(key, extent, jnp.float32) * scale * loudness
    return jnp.minimum(jnp.maximum(entries, -limit), limit).astype(held_as)


def setup_inputs(seed: int = 0) -> dict:
    key_list = jax.random.split(jax.random.key(seed), 3)
    features = scatter_about(key_list[0], (CLIPS, D), 1.0, 6.0, ((0, 256),))
    start_block = scatter_about(key_list[1], (CLIPS, KV), 1.0, 6.0, ((0, 256),), jnp.float32)
    return dict(features=features, start_block=start_block)


kernel_width = 0.04

def normalized(features):
    values = features.astype(jnp.float32)
    factor = 1.0 / jnp.sqrt(lax.optimization_barrier(jnp.sum(values * values, axis=1, keepdims=True)) + 1e-06)
    return (values * factor).astype(jnp.bfloat16)

def kernel_tile(left_rows, left_ids, right_rows, right_ids):
    cosine = lax.dot_general(left_rows.astype(jnp.float32), right_rows.astype(jnp.float32), (((1,), (1,)), ((), ())), preferred_element_type=jnp.float32)
    affinity = jnp.exp((cosine - 1.0) / kernel_width)
    return jnp.where(left_ids[:, None] == right_ids[None, :], jnp.zeros_like(affinity), affinity)

def reference(features, start_block):
    unit_rows = normalized(features)
    count = CLIPS
    row_block = math.gcd(count, 512)
    blocks = count // row_block
    all_ids = jnp.arange(count, dtype=jnp.int32)
    block_list = jnp.arange(blocks, dtype=jnp.int32)

    def tile_of(index):
        first = (index * row_block).astype(jnp.int32)
        rows_here = lax.dynamic_slice_in_dim(unit_rows, first, row_block, 0)
        ids_here = first + jnp.arange(row_block, dtype=jnp.int32)
        return kernel_tile(rows_here, ids_here, unit_rows, all_ids)
    degrees = lax.map(lambda index: lax.optimization_barrier(jnp.sum(tile_of(index), axis=1)), block_list).reshape(count)
    inverse = 1.0 / jnp.sqrt(degrees)
    vectors = start_block
    for sweep_index in range(ITERS):
        scaled = (inverse[:, None] * vectors).astype(jnp.bfloat16)
        product = lax.map(lambda index: jnp.dot(tile_of(index).astype(jnp.bfloat16).astype(jnp.float32), scaled.astype(jnp.float32), preferred_element_type=jnp.float32), block_list).reshape(count, KV)
        image = inverse[:, None] * product
        gram = jnp.dot(image.T.astype(jnp.float32), image.astype(jnp.float32), precision=lax.Precision.HIGHEST, preferred_element_type=jnp.float32)
        lower = jnp.linalg.cholesky(gram)
        vectors = jax.scipy.linalg.solve_triangular(lower, image.T, lower=True).T
    spread = vectors * jnp.sqrt(jnp.float32(count))
    return spread / jnp.sqrt(lax.optimization_barrier(jnp.mean(spread * spread, axis=1, keepdims=True)) + 1e-06)
```

```python
import functools

import jax
import jax.numpy as jnp
from jax import lax
from jax.experimental import pallas as pl
from jax.experimental.pallas import tpu as pltpu
from jax.sharding import PartitionSpec as P

ITERS = 2
KERNEL_WIDTH = 0.04
LOG2E = 1.4426950408889634
MESH = pl.DeviceIdType.MESH

NX, NY, NZ, NC = 4, 4, 8, 2
GROUP = 16
OWN = 64
KV = 128
SLICE = KV // GROUP
CHUNK = 256
F32 = jnp.float32
HIGHEST = lax.Precision.HIGHEST


def spread_of(v, k, axis):
    return jnp.broadcast_to(v[k : k + 1, :] if axis == 0 else v[:, k : k + 1], v.shape)


def inverse_cholesky(rows):
    lane = lax.broadcasted_iota(jnp.int32, (8, KV), 1)
    sub = lax.broadcasted_iota(jnp.int32, (8, KV), 0)
    rows = list(rows)
    out = []
    for p in range(16):
        base = 8 * p
        own = (lane >= base) & (lane < base + 8)
        factors = {i: [spread_of(rows[i], base + k, 1) for k in range(8)] for i in range(p, 16)}
        cols = list(factors[p])
        panel = jnp.where(own, (lane - base == sub).astype(F32), rows[p])
        done = jnp.zeros((8, KV), F32)
        for k in range(8):
            pivot = spread_of(cols[k], k, 0)
            recip = 1.0 / pivot
            at = sub == k
            row = spread_of(panel, k, 0) * recip
            done = jnp.where(at, panel * lax.rsqrt(pivot), done)
            panel = jnp.where(at, row, panel - cols[k] * row)
            for j in range(k + 1, 8):
                entry = spread_of(cols[j], k, 0) * recip
                cols[j] = jnp.where(at, entry, cols[j] - cols[k] * entry)
        out.append(jnp.where(lane <= base + sub, done, 0.0))
        spreads = [spread_of(panel, k, 0) for k in range(8)]
        for i in range(p + 1, 16):
            acc = jnp.where(own, 0.0, rows[i])
            for k in range(8):
                acc = acc - factors[i][k] * spreads[k]
            rows[i] = acc
    return out


(UNIT_ROWS, UNIT_COLS, START, DEGREES, PRODUCT, IMAGE, GRAM_A, GRAM_B, GRAM_C) = range(9)
PER_ITER = 5
STAGES = 4 + ITERS * PER_ITER


def kernel(
    features, start, out,
    unit_rows, unit_cols, tile, start_cols, sums, sums_in, inv_cols, scaled, part, part_in,
    image_cols, gram_part, gram_a, gram_mine, gram_b, gram_c, linv, send, recv,
):
    blk, rep = lax.axis_index("blk"), lax.axis_index("rep")
    x, y, z, c = (rep // 2) * 2 + blk // 32, blk % 4, (blk // 4) % 8, rep % 2
    a, b = z * 2 + c, x * 4 + y

    def device(px, py, pz, pc):
        return ((px % 2) * 32 + pz * 4 + py, (px // 2) * 2 + pc)

    a_peers, b_peers = [], []
    for dz in range(NZ):
        for dc in range(NC):
            if dz or dc:
                pz, pc = (z + dz) % NZ, (c + dc) % NC
                a_peers.append((pz * 2 + pc, device(x, y, pz, pc)))
    for dx in range(NX):
        for dy in range(NY):
            if dx or dy:
                px, py = (x + dx) % NX, (y + dy) % NY
                b_peers.append((px * 4 + py, device(px, py, z, c)))

    barrier = pltpu.get_barrier_semaphore()
    for _, peer in a_peers + b_peers:
        pl.semaphore_signal(barrier, inc=1, device_id=peer, device_id_type=MESH)

    values = features[...].astype(F32)
    factor = 1.0 / jnp.sqrt(jnp.sum(values * values, axis=1, keepdims=True) + 1e-06)
    unit = (values * factor).astype(jnp.bfloat16)
    unit_rows[b] = unit
    unit_cols[a] = unit
    start_cols[a] = start[...]
    pl.semaphore_wait(barrier, len(a_peers) + len(b_peers))

    def copy(stage, src, dst, mine, peer_slot, peer):
        return pltpu.make_async_remote_copy(
            src_ref=src, dst_ref=dst.at[mine], send_sem=send.at[stage, peer_slot],
            recv_sem=recv.at[stage, mine], device_id=peer, device_id_type=MESH,
        )

    def arrive(stage, dst, slot):
        pltpu.make_async_copy(dst.at[slot], dst.at[slot], recv.at[stage, slot]).wait()

    sent = []

    def put(stage, src, dst, mine, peer_slot, peer):
        one = copy(stage, src, dst, mine, peer_slot, peer)
        one.start()
        sent.append(one)

    for slot, peer in b_peers:
        put(UNIT_ROWS, unit_rows.at[b], unit_rows, b, slot, peer)
    sibling = device(x, y, z, 1 - c)
    for dz in range(1, NZ):
        pz = (z + dz) % NZ
        put(UNIT_COLS, unit_cols.at[a], unit_cols, a, pz * 2 + c, device(x, y, pz, c))
    put(UNIT_COLS, unit_cols.at[a], unit_cols, a, z * 2 + 1 - c, sibling)
    for slot, peer in a_peers:
        put(START, start_cols.at[a], start_cols, a, slot, peer)
    for dz in range(1, NZ):
        slot = ((z + dz) % NZ) * 2 + c
        arrive(UNIT_COLS, unit_cols, slot)
        put(UNIT_COLS, unit_cols.at[slot], unit_cols, slot, slot + 1 - 2 * c, sibling)
    for dz in range(0, NZ):
        arrive(UNIT_COLS, unit_cols, ((z + dz) % NZ) * 2 + 1 - c)
    for slot, _ in b_peers:
        arrive(UNIT_ROWS, unit_rows, slot)

    scale = LOG2E / KERNEL_WIDTH
    col_id = lax.broadcasted_iota(jnp.int32, (1, GROUP * OWN), 1) - a * OWN
    col_id = jnp.where((col_id >= 0) & (col_id < OWN), col_id, -1)
    total = jnp.zeros((8, GROUP * OWN), F32)
    for step in range(GROUP * OWN // CHUNK):
        slots = CHUNK // OWN
        rows = unit_rows[step * slots : (step + 1) * slots].reshape(CHUNK, -1)
        cosine = lax.dot_general(
            rows, unit_cols[...].reshape(GROUP * OWN, -1), (((1,), (1,)), ((), ())), preferred_element_type=F32
        )
        row_id = lax.broadcasted_iota(jnp.int32, (CHUNK, 1), 0) + (step * CHUNK - b * OWN)
        row_id = jnp.where((row_id >= 0) & (row_id < OWN), row_id, -2)
        affinity = jnp.where(row_id == col_id, 0.0, jnp.exp2(cosine * scale - scale))
        tile[step * CHUNK : (step + 1) * CHUNK, :] = affinity.astype(jnp.bfloat16)
        total = total + jnp.sum(affinity.reshape(CHUNK // 8, 8, GROUP * OWN), axis=0)
    total = jnp.sum(total, axis=0, keepdims=True)
    for k in range(8):
        sums[k : k + 1, :] = total[:, k * KV : (k + 1) * KV]

    for slot, peer in a_peers:
        put(DEGREES, sums, sums_in, a, slot, peer)
    sums_in[a] = sums[...]
    for slot, _ in a_peers:
        arrive(DEGREES, sums_in, slot)
    inverse = 1.0 / jnp.sqrt(jnp.sum(sums_in[...], axis=0))
    turned = jnp.concatenate([inverse, jnp.zeros((KV - 8, KV), F32)], axis=0).T
    for slot, _ in a_peers:
        arrive(START, start_cols, slot)
    for k in range(8):
        wide = jnp.broadcast_to(turned[:, k : k + 1], (KV, KV))
        inv_cols[k * KV : (k + 1) * KV, :] = wide
        scaled[k * KV : (k + 1) * KV, :] = (
            wide * start_cols[2 * k : 2 * k + 2].reshape(KV, KV)
        ).astype(jnp.bfloat16)
    own_inverse = inv_cols[pl.ds(pl.multiple_of(a * OWN, OWN), OWN), :]

    for it in range(ITERS):
        first = 4 + it * PER_ITER - PRODUCT
        last = it == ITERS - 1
        for step in range(GROUP * OWN // CHUNK):
            product = jnp.dot(
                tile[step * CHUNK : (step + 1) * CHUNK, :], scaled[...], preferred_element_type=F32
            )
            slots = CHUNK // OWN
            part[it, step * slots : (step + 1) * slots] = product.reshape(slots, OWN, KV)
        for slot, peer in b_peers:
            put(first + PRODUCT, part.at[it, slot], part_in.at[it], b, slot, peer)
        part_in[it, b] = part[it, b]
        for slot, _ in b_peers:
            arrive(first + PRODUCT, part_in.at[it], slot)
        image = own_inverse * jnp.sum(part_in[it], axis=0)

        gram = lax.dot_general(
            image, image, (((0,), (0,)), ((), ())), precision=HIGHEST, preferred_element_type=F32
        )
        gram_part[it] = gram.reshape(GROUP, SLICE, KV)
        for slot, peer in b_peers:
            put(first + GRAM_A, gram_part.at[it, slot], gram_a.at[it], b, slot, peer)
        gram_a[it, b] = gram_part[it, b]
        if not last:
            image_cols[a] = image
            for slot, peer in a_peers:
                put(first + IMAGE, image_cols.at[a], image_cols, a, slot, peer)
        for slot, _ in b_peers:
            arrive(first + GRAM_A, gram_a.at[it], slot)
        gram_mine[it] = jnp.sum(gram_a[it], axis=0)
        for slot, peer in a_peers:
            put(first + GRAM_B, gram_mine.at[it], gram_b.at[it], a, slot, peer)
        gram_b[it, a] = gram_mine[it]
        for slot, _ in a_peers:
            arrive(first + GRAM_B, gram_b.at[it], slot)
        gram_c[it, b] = jnp.sum(gram_b[it], axis=0)
        for slot, peer in b_peers:
            put(first + GRAM_C, gram_c.at[it, b], gram_c.at[it], b, slot, peer)
        for slot, _ in b_peers:
            arrive(first + GRAM_C, gram_c.at[it], slot)

        for i, row in enumerate(inverse_cholesky([gram_c[it, i] for i in range(GROUP)])):
            linv[8 * i : 8 * i + 8, :] = row

        def basis(block):
            return lax.dot_general(
                block, linv[...], (((1,), (1,)), ((), ())), precision=HIGHEST, preferred_element_type=F32
            )

        if last:
            spread = basis(image) * jnp.sqrt(F32(NX * NY * NZ * NC * OWN))
            out[...] = spread / jnp.sqrt(jnp.mean(spread * spread, axis=1, keepdims=True) + 1e-06)
        else:
            for slot, _ in a_peers:
                arrive(first + IMAGE, image_cols, slot)
            for step in range(GROUP * OWN // CHUNK):
                slots = CHUNK // OWN
                rows = slice(step * CHUNK, (step + 1) * CHUNK)
                vectors = basis(image_cols[step * slots : (step + 1) * slots].reshape(CHUNK, KV))
                scaled[rows, :] = (inv_cols[rows, :] * vectors).astype(jnp.bfloat16)

    for one in sent:
        one.wait_send()


def body(features, start):
    own, depth = features.shape
    side = GROUP * OWN
    bf16 = jnp.bfloat16
    vmem = pl.BlockSpec(memory_space=pltpu.VMEM)
    return pl.pallas_call(
        kernel,
        out_shape=jax.ShapeDtypeStruct((own, KV), F32),
        in_specs=[vmem, vmem],
        out_specs=vmem,
        scratch_shapes=[
            pltpu.VMEM((GROUP, OWN, depth), bf16),
            pltpu.VMEM((GROUP, OWN, depth), bf16),
            pltpu.VMEM((side, side), bf16),
            pltpu.VMEM((GROUP, OWN, KV), F32),
            pltpu.VMEM((8, KV), F32),
            pltpu.VMEM((GROUP, 8, KV), F32),
            pltpu.VMEM((side, KV), F32),
            pltpu.VMEM((side, KV), bf16),
            pltpu.VMEM((ITERS, GROUP, OWN, KV), F32),
            pltpu.VMEM((ITERS, GROUP, OWN, KV), F32),
            pltpu.VMEM((GROUP, OWN, KV), F32),
            pltpu.VMEM((ITERS, GROUP, SLICE, KV), F32),
            pltpu.VMEM((ITERS, GROUP, SLICE, KV), F32),
            pltpu.VMEM((ITERS, SLICE, KV), F32),
            pltpu.VMEM((ITERS, GROUP, SLICE, KV), F32),
            pltpu.VMEM((ITERS, GROUP, SLICE, KV), F32),
            pltpu.VMEM((KV, KV), F32),
            pltpu.SemaphoreType.DMA((STAGES, GROUP)),
            pltpu.SemaphoreType.DMA((STAGES, GROUP)),
        ],
        compiler_params=pltpu.CompilerParams(
            collective_id=0, has_side_effects=True, vmem_limit_bytes=48 * 2**20
        ),
        name="subspace",
    )(features, start)


def solution(mesh):
    return jax.shard_map(
        body,
        mesh=mesh,
        in_specs=(P(("blk", "rep"), None), P(("blk", "rep"), None)),
        out_specs=P(("blk", "rep"), None),
        check_vma=False,
    )
```

```python
import functools

import jax
import jax.numpy as jnp
from jax import lax
from jax.experimental import pallas as pl
from jax.experimental.pallas import tpu as pltpu
from jax.sharding import PartitionSpec as P

ITERS = 2
KERNEL_WIDTH = 0.04
LOG2E = 1.4426950408889634
MESH = pl.DeviceIdType.MESH

NX, NY, NZ, NC = 4, 4, 8, 2
GROUP = 16
OWN = 64
KV = 128
SLICE = KV // GROUP
CHUNK = 256
F32 = jnp.float32
HIGHEST = lax.Precision.HIGHEST


def spread_of(v, k, axis):
    return jnp.broadcast_to(v[k : k + 1, :] if axis == 0 else v[:, k : k + 1], v.shape)


def inverse_cholesky(rows):
    lane = lax.broadcasted_iota(jnp.int32, (8, KV), 1)
    sub = lax.broadcasted_iota(jnp.int32, (8, KV), 0)
    rows = list(rows)
    out = []
    for p in range(16):
        base = 8 * p
        own = (lane >= base) & (lane < base + 8)
        factors = {i: [spread_of(rows[i], base + k, 1) for k in range(8)] for i in range(p, 16)}
        cols = list(factors[p])
        panel = jnp.where(own, (lane - base == sub).astype(F32), rows[p])
        done = jnp.zeros((8, KV), F32)
        for k in range(8):
            pivot = spread_of(cols[k], k, 0)
            recip = 1.0 / pivot
            at = sub == k
            row = spread_of(panel, k, 0) * recip
            done = jnp.where(at, panel * lax.rsqrt(pivot), done)
            panel = jnp.where(at, row, panel - cols[k] * row)
            for j in range(k + 1, 8):
                entry = spread_of(cols[j], k, 0) * recip
                cols[j] = jnp.where(at, entry, cols[j] - cols[k] * entry)
        out.append(jnp.where(lane <= base + sub, done, 0.0))
        spreads = [spread_of(panel, k, 0) for k in range(8)]
        for i in range(p + 1, 16):
            acc = jnp.where(own, 0.0, rows[i])
            for k in range(8):
                acc = acc - factors[i][k] * spreads[k]
            rows[i] = acc
    return out


(UNIT_Z, UNIT_XY, UNIT_CORE, START, START_CORE, DEGREES) = range(6)
(PRODUCT, GRAM_A, GRAM_B, GRAM_C, IMAGE, IMAGE_CORE) = range(6)
STAGES = 6 + 6 * ITERS
HALF = OWN // 2


def kernel(
    features_hbm, start_hbm, out,
    features, unit_rows, unit_cols, tile, start_cols, sums, sums_in, inv_cols, scaled, part, part_in,
    image_cols, gram_part, gram_a, gram_mine, gram_b, gram_c, linv,
    load, send, recv, ring, first_hop, chunk,
):
    blk, rep = lax.axis_index("blk"), lax.axis_index("rep")
    x, y, z, c = (rep // 2) * 2 + blk // 32, blk % 4, (blk // 4) % 8, rep % 2
    a, b = c * NZ + z, x * NY + y

    def device(px, py, pz, pc):
        return ((px % 2) * 32 + pz * 4 + py, (px // 2) * 2 + pc)

    def shifted(dx, dy, dz, dc):
        return (x + dx) % NX, (y + dy) % NY, (z + dz) % NZ, (c + dc) % NC

    def at(dx=0, dy=0, dz=0, dc=0):
        return device(*shifted(dx, dy, dz, dc))

    far_first = (2, 1, 3)
    near_first = (1, 3, 2)
    sibling = at(dc=1)
    barrier = pltpu.get_barrier_semaphore()
    near = [at(dx=d) for d in near_first] + [at(dy=d) for d in near_first] + [at(dz=1), at(dz=NZ - 1), sibling]
    for peer in near:
        pl.semaphore_signal(barrier, inc=1, device_id=peer, device_id_type=MESH)
    load_features = pltpu.make_async_copy(features_hbm, features, load.at[0])
    load_features.start()
    load_start = pltpu.make_async_copy(start_hbm, start_cols.at[a], load.at[1])
    load_start.start()

    load_features.wait()
    values = features[...].astype(F32)
    factor = 1.0 / jnp.sqrt(jnp.sum(values * values, axis=1, keepdims=True) + 1e-06)
    unit = (values * factor).astype(jnp.bfloat16).reshape(2, HALF, -1)
    unit_rows[pl.ds(2 * b, 2)] = unit
    unit_cols[pl.ds(2 * a, 2)] = unit
    pl.semaphore_wait(barrier, len(near))

    def put(src, dst, stage, arrival, peer):
        pltpu.make_async_remote_copy(
            src_ref=src, dst_ref=dst, send_sem=send.at[stage], recv_sem=arrival,
            device_id=peer, device_id_type=MESH,
        ).start()

    def wait_for(ref, semaphore):
        pltpu.make_async_copy(ref, ref, semaphore).wait()

    def put_row_half(px, py, h, peer, arrival):
        half = unit_rows.at[2 * (px * NY + py) + h]
        put(half, half, UNIT_XY, arrival, peer)

    def put_col_half(pz, pc, h, peer, stage, arrival):
        half = unit_cols.at[2 * (pc * NZ + pz) + h]
        put(half, half, stage, arrival, peer)

    for h in range(2):
        put_col_half(z, c, h, at(dz=1), UNIT_Z, ring.at[0, 0, h])
        put_col_half(z, c, h, at(dz=NZ - 1), UNIT_Z, ring.at[1, 0, h])
        for d in near_first:
            if h == 0:
                put_row_half(x, y, 0, at(dx=d), first_hop.at[0, NX - d])
                put_row_half(x, y, 1, at(dy=d), first_hop.at[1, NY - d])
            else:
                put_row_half(x, y, 1, at(dx=d), chunk.at[NX - d])
                put_row_half(x, y, 0, at(dy=d), chunk.at[0])
    for h in range(2):
        put_col_half(z, c, h, sibling, UNIT_CORE, recv.at[UNIT_CORE])

    def ring_step(way, d, h):
        pz = (z - d) % NZ if way == 0 else (z + d) % NZ
        half = unit_cols.at[2 * (c * NZ + pz) + h]
        wait_for(half, ring.at[way, d - 1, h])
        if d < 3 or (d == 3 and h == way):
            put_col_half(pz, c, h, at(dz=1 if way == 0 else NZ - 1), UNIT_Z, ring.at[way, d, h])
        put_col_half(pz, c, h, sibling, UNIT_CORE, recv.at[UNIT_CORE])

    def plane_step(d):
        px = (x + d) % NX
        wait_for(unit_rows.at[2 * (px * NY + y)], first_hop.at[0, d])
        for e in near_first:
            put_row_half(px, y, 0, at(dy=e), chunk.at[d])
        py = (y + d) % NY
        wait_for(unit_rows.at[2 * (x * NY + py) + 1], first_hop.at[1, d])
        for e in near_first:
            put_row_half(x, py, 1, at(dx=e), chunk.at[NX - e])

    for h in range(2):
        for way in range(2):
            ring_step(way, 1, h)
    plane_step(1)
    plane_step(3)
    for h in range(2):
        for way in range(2):
            ring_step(way, 2, h)
    plane_step(2)
    for h in range(2):
        for way in range(2):
            ring_step(way, 3, h)
    for way in range(2):
        ring_step(way, 4, way)

    load_start.wait()
    along_z = (1, 7, 2, 6, 3, 5, 4)
    for d in along_z:
        put(start_cols.at[a], start_cols.at[a], START, recv.at[START], at(dz=d))

    wait_for(unit_cols.at[pl.ds(0, 2 * NZ)], recv.at[UNIT_CORE])
    scale = LOG2E / KERNEL_WIDTH
    side = GROUP * OWN
    col_id = lax.broadcasted_iota(jnp.int32, (1, side), 1) - a * OWN
    col_id = jnp.where((col_id >= 0) & (col_id < OWN), col_id, -1)
    total = jnp.zeros((8, side), F32)
    for d in (0,) + near_first:
        px = (x + d) % NX
        wait_for(unit_rows.at[pl.ds(0, 7 if d else 3)], chunk.at[d])
        rows = unit_rows[pl.ds(px * 2 * NY, 2 * NY)].reshape(CHUNK, -1)
        cosine = lax.dot_general(
            rows, unit_cols[...].reshape(side, -1), (((1,), (1,)), ((), ())), preferred_element_type=F32
        )
        if d == 0:
            row_id = lax.broadcasted_iota(jnp.int32, (CHUNK, 1), 0) - y * OWN
            row_id = jnp.where((row_id >= 0) & (row_id < OWN), row_id, -2)
            affinity = jnp.where(row_id == col_id, 0.0, jnp.exp2(cosine * scale - scale))
        else:
            affinity = jnp.exp2(cosine * scale - scale)
        tile[pl.ds(pl.multiple_of(px * CHUNK, CHUNK), CHUNK), :] = affinity.astype(jnp.bfloat16)
        total = total + jnp.sum(affinity.reshape(CHUNK // 8, 8, side), axis=0)
    total = jnp.sum(total, axis=0, keepdims=True)
    for k in range(8):
        sums[k : k + 1, :] = total[:, k * KV : (k + 1) * KV]

    a_peers = [at(dz=d, dc=e) for d in along_z for e in range(NC)] + [sibling]
    b_shifts = [(dx, dy) for dx in (2, 1, 3, 0) for dy in (2, 1, 3, 0) if dx or dy]
    for peer in a_peers:
        put(sums, sums_in.at[a], DEGREES, recv.at[DEGREES], peer)
    sums_in[a] = sums[...]
    wait_for(start_cols.at[pl.ds(0, NZ - 1)], recv.at[START])
    mine = pl.ds(c * NZ, NZ)
    put(start_cols.at[mine], start_cols.at[mine], START_CORE, recv.at[START_CORE], sibling)
    wait_for(sums_in.at[pl.ds(0, GROUP - 1)], recv.at[DEGREES])
    inverse = 1.0 / jnp.sqrt(jnp.sum(sums_in[...], axis=0))
    turned = jnp.concatenate([inverse, jnp.zeros((KV - 8, KV), F32)], axis=0).T
    wait_for(start_cols.at[pl.ds(0, NZ)], recv.at[START_CORE])
    for k in range(8):
        wide = jnp.broadcast_to(turned[:, k : k + 1], (KV, KV))
        inv_cols[k * KV : (k + 1) * KV, :] = wide
        scaled[k * KV : (k + 1) * KV, :] = (
            wide * start_cols[2 * k : 2 * k + 2].reshape(KV, KV)
        ).astype(jnp.bfloat16)
    own_inverse = inv_cols[pl.ds(pl.multiple_of(a * OWN, OWN), OWN), :]

    for it in range(ITERS):
        first = 6 + 6 * it
        last = it == ITERS - 1
        slots = CHUNK // OWN
        for dx in (2, 1, 3, 0):
            px = (x + dx) % NX
            product = jnp.dot(
                tile[pl.ds(pl.multiple_of(px * CHUNK, CHUNK), CHUNK), :], scaled[...], preferred_element_type=F32
            )
            part[it, pl.ds(px * slots, slots)] = product.reshape(slots, OWN, KV)
            for dy in (2, 1, 3, 0):
                if dx or dy:
                    py = (y + dy) % NY
                    put(
                        part.at[it, px * NY + py], part_in.at[it, b], first + PRODUCT,
                        recv.at[first + PRODUCT], at(dx=dx, dy=dy),
                    )
        part_in[it, b] = part[it, b]
        wait_for(part_in.at[it, pl.ds(0, GROUP - 1)], recv.at[first + PRODUCT])
        image = own_inverse * jnp.sum(part_in[it], axis=0)
        if not last:
            image_cols[a] = image
        gram = lax.dot_general(
            image, image, (((0,), (0,)), ((), ())), precision=HIGHEST, preferred_element_type=F32
        )
        gram_part[it] = gram.reshape(GROUP, SLICE, KV)
        for dx, dy in b_shifts:
            px, py, _, _ = shifted(dx, dy, 0, 0)
            put(
                gram_part.at[it, px * NY + py], gram_a.at[it, b], first + GRAM_A,
                recv.at[first + GRAM_A], at(dx=dx, dy=dy),
            )
        gram_a[it, b] = gram_part[it, b]
        wait_for(gram_a.at[it, pl.ds(0, GROUP - 1)], recv.at[first + GRAM_A])
        gram_mine[it] = jnp.sum(gram_a[it], axis=0)
        for peer in a_peers:
            put(gram_mine.at[it], gram_b.at[it, a], first + GRAM_B, recv.at[first + GRAM_B], peer)
        if not last:
            for d in along_z:
                put(image_cols.at[a], image_cols.at[a], first + IMAGE, recv.at[first + IMAGE], at(dz=d))
        gram_b[it, a] = gram_mine[it]
        wait_for(gram_b.at[it, pl.ds(0, GROUP - 1)], recv.at[first + GRAM_B])
        gram_c[it, b] = jnp.sum(gram_b[it], axis=0)
        for dx, dy in b_shifts:
            put(
                gram_c.at[it, b], gram_c.at[it, b], first + GRAM_C, recv.at[first + GRAM_C], at(dx=dx, dy=dy)
            )
        wait_for(gram_c.at[it, pl.ds(0, GROUP - 1)], recv.at[first + GRAM_C])
        if not last:
            wait_for(image_cols.at[pl.ds(0, NZ - 1)], recv.at[first + IMAGE])
            put(
                image_cols.at[mine], image_cols.at[mine], first + IMAGE_CORE, recv.at[first + IMAGE_CORE], sibling
            )

        for i, row in enumerate(inverse_cholesky([gram_c[it, i] for i in range(GROUP)])):
            linv[8 * i : 8 * i + 8, :] = row

        def basis(block):
            return lax.dot_general(
                block, linv[...], (((1,), (1,)), ((), ())), precision=HIGHEST, preferred_element_type=F32
            )

        if last:
            spread = basis(image) * jnp.sqrt(F32(NX * NY * NZ * NC * OWN))
            out[...] = spread / jnp.sqrt(jnp.mean(spread * spread, axis=1, keepdims=True) + 1e-06)
        else:
            wait_for(image_cols.at[pl.ds(0, NZ)], recv.at[first + IMAGE_CORE])
            for step in range(GROUP * OWN // CHUNK):
                rows = slice(step * CHUNK, (step + 1) * CHUNK)
                vectors = basis(image_cols[step * slots : (step + 1) * slots].reshape(CHUNK, KV))
                scaled[rows, :] = (inv_cols[rows, :] * vectors).astype(jnp.bfloat16)

    wait_for(unit_cols.at[pl.ds(0, 14)], send.at[UNIT_Z])
    wait_for(unit_cols.at[pl.ds(0, 16)], send.at[UNIT_CORE])
    wait_for(unit_rows.at[pl.ds(0, 30)], send.at[UNIT_XY])
    wait_for(start_cols.at[pl.ds(0, NZ - 1)], send.at[START])
    wait_for(start_cols.at[pl.ds(0, NZ)], send.at[START_CORE])
    wait_for(sums_in.at[pl.ds(0, GROUP - 1)], send.at[DEGREES])
    for it in range(ITERS):
        first = 6 + 6 * it
        wait_for(part.at[it, pl.ds(0, GROUP - 1)], send.at[first + PRODUCT])
        for stage in (GRAM_A, GRAM_B, GRAM_C):
            wait_for(gram_a.at[it, pl.ds(0, GROUP - 1)], send.at[first + stage])
        if it < ITERS - 1:
            wait_for(image_cols.at[pl.ds(0, NZ - 1)], send.at[first + IMAGE])
            wait_for(image_cols.at[pl.ds(0, NZ)], send.at[first + IMAGE_CORE])


def body(features, start):
    own, depth = features.shape
    side = GROUP * OWN
    bf16 = jnp.bfloat16
    hbm = pl.BlockSpec(memory_space=pl.ANY)
    dma = pltpu.SemaphoreType.DMA
    return pl.pallas_call(
        kernel,
        out_shape=jax.ShapeDtypeStruct((own, KV), F32),
        in_specs=[hbm, hbm],
        out_specs=pl.BlockSpec(memory_space=pltpu.VMEM),
        scratch_shapes=[
            pltpu.VMEM((own, depth), bf16),
            pltpu.VMEM((2 * GROUP, HALF, depth), bf16),
            pltpu.VMEM((2 * GROUP, HALF, depth), bf16),
            pltpu.VMEM((side, side), bf16),
            pltpu.VMEM((GROUP, OWN, KV), F32),
            pltpu.VMEM((8, KV), F32),
            pltpu.VMEM((GROUP, 8, KV), F32),
            pltpu.VMEM((side, KV), F32),
            pltpu.VMEM((side, KV), bf16),
            pltpu.VMEM((ITERS, GROUP, OWN, KV), F32),
            pltpu.VMEM((ITERS, GROUP, OWN, KV), F32),
            pltpu.VMEM((GROUP, OWN, KV), F32),
            pltpu.VMEM((ITERS, GROUP, SLICE, KV), F32),
            pltpu.VMEM((ITERS, GROUP, SLICE, KV), F32),
            pltpu.VMEM((ITERS, SLICE, KV), F32),
            pltpu.VMEM((ITERS, GROUP, SLICE, KV), F32),
            pltpu.VMEM((ITERS, GROUP, SLICE, KV), F32),
            pltpu.VMEM((KV, KV), F32),
            dma((2,)),
            dma((STAGES,)),
            dma((STAGES,)),
            dma((2, 4, 2)),
            dma((2, 4)),
            dma((4,)),
        ],
        compiler_params=pltpu.CompilerParams(
            collective_id=0, has_side_effects=True, vmem_limit_bytes=48 * 2**20
        ),
        name="subspace",
    )(features, start)


def solution(mesh):
    return jax.shard_map(
        body,
        mesh=mesh,
        in_specs=(P(("blk", "rep"), None), P(("blk", "rep"), None)),
        out_specs=P(("blk", "rep"), None),
        check_vma=False,
    )
```

```python
import functools

import jax
import jax.numpy as jnp
from jax import lax
from jax.experimental import pallas as pl
from jax.experimental.pallas import tpu as pltpu
from jax.sharding import PartitionSpec as P

ITERS = 2
KERNEL_WIDTH = 0.04
LOG2E = 1.4426950408889634
MESH = pl.DeviceIdType.MESH

NX, NY, NZ, NC = 4, 4, 8, 2
GROUP = 16
OWN = 64
KV = 128
SLICE = KV // GROUP
CHUNK = 256
F32 = jnp.float32
HIGHEST = lax.Precision.HIGHEST


def spread_of(v, k, axis):
    return jnp.broadcast_to(v[k : k + 1, :] if axis == 0 else v[:, k : k + 1], v.shape)


def inverse_cholesky(rows):
    lane = lax.broadcasted_iota(jnp.int32, (8, KV), 1)
    sub = lax.broadcasted_iota(jnp.int32, (8, KV), 0)
    rows = list(rows)
    out = []
    for p in range(16):
        base = 8 * p
        own = (lane >= base) & (lane < base + 8)
        cols = [spread_of(rows[p], base + k, 1) for k in range(8)]
        panel = jnp.where(own, (lane - base == sub).astype(F32), rows[p])
        done = jnp.zeros((8, KV), F32)
        scale = jnp.ones((8, KV), F32)
        for k in range(8):
            pivot = spread_of(cols[k], k, 0)
            recip = 1.0 / pivot
            here = sub == k
            others = jnp.where(here, 0.0, cols[k])
            for j in range(k + 1, 8):
                cols[j] = cols[j] - (others * spread_of(cols[j], k, 0)) * recip
            done = jnp.where(here, panel * lax.rsqrt(pivot), done)
            scale = jnp.where(here, recip, scale)
            panel = panel - (others * spread_of(panel, k, 0)) * recip
        panel = panel * scale
        out.append(jnp.where(lane <= base + sub, done, 0.0))
        spreads = [spread_of(panel, k, 0) for k in range(8)]
        for i in range(p + 1, 16):
            acc = jnp.where(own, 0.0, rows[i])
            for k in range(8):
                acc = acc - spread_of(rows[i], base + k, 1) * spreads[k]
            rows[i] = acc
    return out


(UNIT_Z, UNIT_XY, UNIT_CORE, START_Z, START_CORE, DEGREES) = range(6)
(PRODUCT, GRAM_A, GRAM_B, GRAM_C, IMAGE_Z, IMAGE_FAR, IMAGE_CORE) = range(7)
STAGES = 6 + 7 * ITERS
HALF = OWN // 2


def kernel(
    features_hbm, start_hbm, out,
    features, unit_rows, unit_cols, tile, start_cols, sums, sums_in, inv_cols, scaled, part, part_in,
    image_cols, gram_part, gram_a, gram_mine, gram_b, gram_c, linv,
    load, send, recv, unit_ring, start_ring, image_ring, first_hop, chunk,
):
    blk, rep = lax.axis_index("blk"), lax.axis_index("rep")
    x, y, z, c = (rep // 2) * 2 + blk // 32, blk % 4, (blk // 4) % 8, rep % 2
    a, b = c * NZ + z, x * NY + y

    def device(px, py, pz, pc):
        return ((px % 2) * 32 + pz * 4 + py, (px // 2) * 2 + pc)

    def shifted(dx, dy, dz, dc):
        return (x + dx) % NX, (y + dy) % NY, (z + dz) % NZ, (c + dc) % NC

    def at(dx=0, dy=0, dz=0, dc=0):
        return device(*shifted(dx, dy, dz, dc))

    far_first = (2, 1, 3)
    near_first = (1, 3, 2)
    sibling = at(dc=1)
    barrier = pltpu.get_barrier_semaphore()
    way = 1 - 2 * c
    following, preceding = at(dz=way + NZ), at(dz=NZ - way)
    near = [at(dx=d) for d in near_first] + [at(dy=d) for d in near_first] + [sibling]
    for peer in near + [preceding]:
        pl.semaphore_signal(barrier, inc=1, device_id=peer, device_id_type=MESH)
    load_features = pltpu.make_async_copy(features_hbm, features, load.at[0])
    load_features.start()
    load_start = pltpu.make_async_copy(start_hbm, start_cols.at[a], load.at[1])
    load_start.start()

    load_features.wait()
    values = features[...].astype(F32)
    factor = 1.0 / jnp.sqrt(jnp.sum(values * values, axis=1, keepdims=True) + 1e-06)
    unit = (values * factor).astype(jnp.bfloat16).reshape(2, HALF, -1)
    unit_rows[pl.ds(2 * b, 2)] = unit
    unit_cols[pl.ds(2 * a, 2)] = unit
    pl.semaphore_wait(barrier, len(near) + 1)

    def put(src, dst, stage, arrival, peer):
        pltpu.make_async_remote_copy(
            src_ref=src, dst_ref=dst, send_sem=send.at[stage], recv_sem=arrival,
            device_id=peer, device_id_type=MESH,
        ).start()

    def wait_for(ref, semaphore):
        pltpu.make_async_copy(ref, ref, semaphore).wait()

    def put_row_half(px, py, h, peer, arrival):
        half = unit_rows.at[2 * (px * NY + py) + h]
        put(half, half, UNIT_XY, arrival, peer)

    def hand_on(array, slot, ring, d, other, stage_z, stage_core):
        block = array.at[slot]
        if d or other:
            wait_for(block, ring.at[d, other])
        if d < 3 or (d == 3 and not other):
            put(block, block, stage_z, ring.at[d + 1, other], following)
        if not (d or other):
            put(block, block, stage_core, ring.at[0, 1], sibling)
        elif d:
            put(block, block, stage_core, recv.at[stage_core], sibling)

    def unit_step(d, other):
        slot = ((c + other) % NC) * NZ + (z - d * way) % NZ
        for h in range(2):
            hand_on(unit_cols, 2 * slot + h, unit_ring.at[h], d, other, UNIT_Z, UNIT_CORE)

    def start_step(d, other):
        slot = ((c + other) % NC) * NZ + (z - d * way) % NZ
        hand_on(start_cols, slot, start_ring, d, other, START_Z, START_CORE)

    def plane_step(d):
        px = (x + d) % NX
        wait_for(unit_rows.at[2 * (px * NY + y)], first_hop.at[0, d])
        for e in near_first:
            put_row_half(px, y, 0, at(dy=e), chunk.at[d])
        py = (y + d) % NY
        wait_for(unit_rows.at[2 * (x * NY + py) + 1], first_hop.at[1, d])
        for e in near_first:
            put_row_half(x, py, 1, at(dx=e), chunk.at[NX - e])

    unit_step(0, 0)
    for d in near_first:
        put_row_half(x, y, 0, at(dx=d), first_hop.at[0, NX - d])
        put_row_half(x, y, 1, at(dy=d), first_hop.at[1, NY - d])
    unit_step(0, 1)
    load_start.wait()
    start_step(0, 0)
    for d in near_first:
        put_row_half(x, y, 1, at(dx=d), chunk.at[NX - d])
        put_row_half(x, y, 0, at(dy=d), chunk.at[0])
    for d in range(1, 4):
        unit_step(d, 0)
        plane_step((1, 3, 2)[d - 1])
        unit_step(d, 1)
        if d > 1:
            start_step(d - 1, 0)
        start_step(d - 1, 1)
    unit_step(4, 0)

    wait_for(unit_cols.at[pl.ds(0, 2 * (NZ - 1))], recv.at[UNIT_CORE])
    scale = LOG2E / KERNEL_WIDTH
    side = GROUP * OWN
    col_id = lax.broadcasted_iota(jnp.int32, (1, side), 1) - a * OWN
    col_id = jnp.where((col_id >= 0) & (col_id < OWN), col_id, -1)
    total = jnp.zeros((8, side), F32)
    for d in (0,) + near_first:
        px = (x + d) % NX
        wait_for(unit_rows.at[pl.ds(0, 7 if d else 3)], chunk.at[d])
        rows = unit_rows[pl.ds(px * 2 * NY, 2 * NY)].reshape(CHUNK, -1)
        cosine = lax.dot_general(
            rows, unit_cols[...].reshape(side, -1), (((1,), (1,)), ((), ())), preferred_element_type=F32
        )
        if d == 0:
            row_id = lax.broadcasted_iota(jnp.int32, (CHUNK, 1), 0) - y * OWN
            row_id = jnp.where((row_id >= 0) & (row_id < OWN), row_id, -2)
            affinity = jnp.where(row_id == col_id, 0.0, jnp.exp2(cosine * scale - scale))
        else:
            affinity = jnp.exp2(cosine * scale - scale)
        tile[pl.ds(pl.multiple_of(px * CHUNK, CHUNK), CHUNK), :] = affinity.astype(jnp.bfloat16)
        total = total + jnp.sum(affinity.reshape(CHUNK // 8, 8, side), axis=0)
        if d == 0:
            start_step(3, 0)
            start_step(3, 1)
    total = jnp.sum(total, axis=0, keepdims=True)
    for k in range(8):
        sums[k : k + 1, :] = total[:, k * KV : (k + 1) * KV]

    along_z = (4, 5, 3, 6, 2, 7, 1)
    a_peers = [at(dz=d, dc=e) for d in along_z for e in range(NC)] + [sibling]
    b_shifts = [(dx, dy) for dx in (2, 1, 3, 0) for dy in (2, 1, 3, 0) if dx or dy]
    for peer in a_peers:
        put(sums, sums_in.at[a], DEGREES, recv.at[DEGREES], peer)
    sums_in[a] = sums[...]
    start_step(4, 0)
    wait_for(sums_in.at[pl.ds(0, GROUP - 1)], recv.at[DEGREES])
    inverse = 1.0 / jnp.sqrt(jnp.sum(sums_in[...], axis=0))
    turned = jnp.concatenate([inverse, jnp.zeros((KV - 8, KV), F32)], axis=0).T
    wait_for(start_cols.at[pl.ds(0, NZ - 1)], recv.at[START_CORE])
    for k in range(8):
        wide = jnp.broadcast_to(turned[:, k : k + 1], (KV, KV))
        inv_cols[k * KV : (k + 1) * KV, :] = wide
        scaled[k * KV : (k + 1) * KV, :] = (
            wide * start_cols[2 * k : 2 * k + 2].reshape(KV, KV)
        ).astype(jnp.bfloat16)
    own_inverse = inv_cols[pl.ds(pl.multiple_of(a * OWN, OWN), OWN), :]

    def image_step(first, d):
        blocks = {1: image_cols.at[c * NZ + (z - d) % NZ], NZ - 1: image_cols.at[c * NZ + (z + d) % NZ]}
        for i, (ahead, block) in enumerate(blocks.items()):
            if d:
                wait_for(block, image_ring.at[i, d])
            if d < 3:
                put(block, block, first + IMAGE_Z, image_ring.at[i, d + 1], at(dz=ahead))
            elif ahead == 1:
                for e in range(NC):
                    put(block, block, first + IMAGE_FAR, recv.at[first + IMAGE_FAR], at(dz=1, dc=e))
            if d or not i:
                put(block, block, first + IMAGE_CORE, recv.at[first + IMAGE_CORE], sibling)

    for it in range(ITERS):
        first = 6 + 7 * it
        last = it == ITERS - 1
        slots = CHUNK // OWN
        for dx in (2, 1, 3, 0):
            px = (x + dx) % NX
            product = jnp.dot(
                tile[pl.ds(pl.multiple_of(px * CHUNK, CHUNK), CHUNK), :], scaled[...], preferred_element_type=F32
            )
            part[it, pl.ds(px * slots, slots)] = product.reshape(slots, OWN, KV)
            for dy in (2, 1, 3, 0):
                if dx or dy:
                    py = (y + dy) % NY
                    put(
                        part.at[it, px * NY + py], part_in.at[it, b], first + PRODUCT,
                        recv.at[first + PRODUCT], at(dx=dx, dy=dy),
                    )
        part_in[it, b] = part[it, b]
        wait_for(part_in.at[it, pl.ds(0, GROUP - 1)], recv.at[first + PRODUCT])
        image = own_inverse * jnp.sum(part_in[it], axis=0)
        if not last:
            image_cols[a] = image
            image_step(first, 0)
        gram = lax.dot_general(
            image, image, (((0,), (0,)), ((), ())), precision=HIGHEST, preferred_element_type=F32
        )
        gram_part[it] = gram.reshape(GROUP, SLICE, KV)
        for dx, dy in b_shifts:
            px, py, _, _ = shifted(dx, dy, 0, 0)
            put(
                gram_part.at[it, px * NY + py], gram_a.at[it, b], first + GRAM_A,
                recv.at[first + GRAM_A], at(dx=dx, dy=dy),
            )
        gram_a[it, b] = gram_part[it, b]
        wait_for(gram_a.at[it, pl.ds(0, GROUP - 1)], recv.at[first + GRAM_A])
        gram_mine[it] = jnp.sum(gram_a[it], axis=0)
        for peer in a_peers:
            put(gram_mine.at[it], gram_b.at[it, a], first + GRAM_B, recv.at[first + GRAM_B], peer)
        if not last:
            image_step(first, 1)
        gram_b[it, a] = gram_mine[it]
        wait_for(gram_b.at[it, pl.ds(0, GROUP - 1)], recv.at[first + GRAM_B])
        gram_c[it, b] = jnp.sum(gram_b[it], axis=0)
        for dx, dy in b_shifts:
            put(
                gram_c.at[it, b], gram_c.at[it, b], first + GRAM_C, recv.at[first + GRAM_C], at(dx=dx, dy=dy)
            )
        if not last:
            image_step(first, 2)
        wait_for(gram_c.at[it, pl.ds(0, GROUP - 1)], recv.at[first + GRAM_C])
        if not last:
            image_step(first, 3)

        for i, row in enumerate(inverse_cholesky([gram_c[it, i] for i in range(GROUP)])):
            linv[8 * i : 8 * i + 8, :] = row

        def basis(block):
            return lax.dot_general(
                block, linv[...], (((1,), (1,)), ((), ())), precision=HIGHEST, preferred_element_type=F32
            )

        if last:
            vectors = basis(image)
            spread = vectors * jnp.sqrt(F32(NX * NY * NZ * NC * OWN))
            out[...] = vectors / jnp.sqrt(jnp.mean(spread * spread, axis=1, keepdims=True) + 1e-06)
        else:
            wait_for(image_cols.at[pl.ds(0, NZ - 1)], recv.at[first + IMAGE_CORE])
            wait_for(image_cols.at[pl.ds(0, NC)], recv.at[first + IMAGE_FAR])
            for step in range(GROUP * OWN // CHUNK):
                rows = slice(step * CHUNK, (step + 1) * CHUNK)
                vectors = basis(image_cols[step * slots : (step + 1) * slots].reshape(CHUNK, KV))
                scaled[rows, :] = (inv_cols[rows, :] * vectors).astype(jnp.bfloat16)

    wait_for(unit_cols.at[pl.ds(0, 14)], send.at[UNIT_Z])
    wait_for(unit_cols.at[pl.ds(0, 16)], send.at[UNIT_CORE])
    wait_for(start_cols.at[pl.ds(0, 7)], send.at[START_Z])
    wait_for(start_cols.at[pl.ds(0, 8)], send.at[START_CORE])
    wait_for(unit_rows.at[pl.ds(0, 30)], send.at[UNIT_XY])
    wait_for(sums_in.at[pl.ds(0, GROUP - 1)], send.at[DEGREES])
    for it in range(ITERS):
        first = 6 + 7 * it
        wait_for(part.at[it, pl.ds(0, GROUP - 1)], send.at[first + PRODUCT])
        for stage in (GRAM_A, GRAM_B, GRAM_C):
            wait_for(gram_a.at[it, pl.ds(0, GROUP - 1)], send.at[first + stage])
        if it < ITERS - 1:
            wait_for(image_cols.at[pl.ds(0, 6)], send.at[first + IMAGE_Z])
            wait_for(image_cols.at[pl.ds(0, 2)], send.at[first + IMAGE_FAR])
            wait_for(image_cols.at[pl.ds(0, 7)], send.at[first + IMAGE_CORE])


def body(features, start):
    own, depth = features.shape
    side = GROUP * OWN
    bf16 = jnp.bfloat16
    hbm = pl.BlockSpec(memory_space=pl.ANY)
    dma = pltpu.SemaphoreType.DMA
    unscaled = pl.pallas_call(
        kernel,
        out_shape=jax.ShapeDtypeStruct((own, KV), F32),
        in_specs=[hbm, hbm],
        out_specs=pl.BlockSpec(memory_space=pltpu.VMEM),
        scratch_shapes=[
            pltpu.VMEM((own, depth), bf16),
            pltpu.VMEM((2 * GROUP, HALF, depth), bf16),
            pltpu.VMEM((2 * GROUP, HALF, depth), bf16),
            pltpu.VMEM((side, side), bf16),
            pltpu.VMEM((GROUP, OWN, KV), F32),
            pltpu.VMEM((8, KV), F32),
            pltpu.VMEM((GROUP, 8, KV), F32),
            pltpu.VMEM((side, KV), F32),
            pltpu.VMEM((side, KV), bf16),
            pltpu.VMEM((ITERS, GROUP, OWN, KV), F32),
            pltpu.VMEM((ITERS, GROUP, OWN, KV), F32),
            pltpu.VMEM((GROUP, OWN, KV), F32),
            pltpu.VMEM((ITERS, GROUP, SLICE, KV), F32),
            pltpu.VMEM((ITERS, GROUP, SLICE, KV), F32),
            pltpu.VMEM((ITERS, SLICE, KV), F32),
            pltpu.VMEM((ITERS, GROUP, SLICE, KV), F32),
            pltpu.VMEM((ITERS, GROUP, SLICE, KV), F32),
            pltpu.VMEM((KV, KV), F32),
            dma((2,)),
            dma((STAGES,)),
            dma((STAGES,)),
            dma((2, 5, 2)),
            dma((5, 2)),
            dma((2, 4)),
            dma((2, 4)),
            dma((4,)),
        ],
        compiler_params=pltpu.CompilerParams(
            collective_id=0, has_side_effects=True, vmem_limit_bytes=55200 * 1024
        ),
        name="subspace",
    )(features, start)
    return unscaled * jnp.sqrt(F32(NX * NY * NZ * NC * OWN))


def solution(mesh):
    return jax.shard_map(
        body,
        mesh=mesh,
        in_specs=(P(("blk", "rep"), None), P(("blk", "rep"), None)),
        out_specs=P(("blk", "rep"), None),
        check_vma=False,
    )
```

```python
import functools

import jax
import jax.numpy as jnp
from jax import lax
from jax.experimental import pallas as pl
from jax.experimental.pallas import tpu as pltpu
from jax.sharding import PartitionSpec as P

ITERS = 2
KERNEL_WIDTH = 0.04
LOG2E = 1.4426950408889634
MESH = pl.DeviceIdType.MESH

NX, NY, NZ, NC = 4, 4, 8, 2
GROUP = 16
OWN = 64
KV = 128
SLICE = KV // GROUP
CHUNK = 256
F32 = jnp.float32
HIGHEST = lax.Precision.HIGHEST


def spread_of(v, k, axis):
    return jnp.broadcast_to(v[k : k + 1, :] if axis == 0 else v[:, k : k + 1], v.shape)


def inverse_cholesky(rows):
    lane = lax.broadcasted_iota(jnp.int32, (8, KV), 1)
    sub = lax.broadcasted_iota(jnp.int32, (8, KV), 0)
    rows = list(rows)
    out = []
    for p in range(16):
        base = 8 * p
        own = (lane >= base) & (lane < base + 8)
        cols = [spread_of(rows[p], base + k, 1) for k in range(8)]
        panel = jnp.where(own, (lane - base == sub).astype(F32), rows[p])
        done = jnp.zeros((8, KV), F32)
        scale = jnp.ones((8, KV), F32)
        for k in range(8):
            pivot = spread_of(cols[k], k, 0)
            recip = 1.0 / pivot
            here = sub == k
            others = jnp.where(here, 0.0, cols[k])
            for j in range(k + 1, 8):
                cols[j] = cols[j] - (others * spread_of(cols[j], k, 0)) * recip
            done = jnp.where(here, panel * lax.rsqrt(pivot), done)
            scale = jnp.where(here, recip, scale)
            panel = panel - (others * spread_of(panel, k, 0)) * recip
        panel = panel * scale
        out.append(jnp.where(lane <= base + sub, done, 0.0))
        spreads = [spread_of(panel, k, 0) for k in range(8)]
        for i in range(p + 1, 16):
            acc = jnp.where(own, 0.0, rows[i])
            for k in range(8):
                acc = acc - spread_of(rows[i], base + k, 1) * spreads[k]
            rows[i] = acc
    return out


(UNIT_XY, UNIT_Z, UNIT_FAR, UNIT_CORE, UNIT_CORE_FAR, START_Z, START_FAR, START_CORE, DEGREES) = range(9)
(PRODUCT, GRAM_A, GRAM_B, GRAM_C, IMAGE_Z, IMAGE_FAR, IMAGE_CORE) = range(7)
STAGES = 9 + 7 * ITERS
COL_ORDER = (0, 1, 7, 2, 6, 3, 5, 4)
NEAR_COLS = 5 * NC * OWN
HALF = OWN // 2


def kernel(
    features_hbm, start_hbm, out,
    features, unit_rows, unit_cols, tile, start_cols, sums, sums_in, inverses, inv_cols, scaled, part, part_in,
    image_cols, gram_part, gram_a, gram_mine, gram_b, gram_c, linv,
    load, send, recv, unit_ring, start_ring, image_ring, first_hop, chunk,
):
    blk, rep = lax.axis_index("blk"), lax.axis_index("rep")
    x, y, z, c = (rep // 2) * 2 + blk // 32, blk % 4, (blk // 4) % 8, rep % 2
    a, b = c * NZ + z, x * NY + y

    def device(px, py, pz, pc):
        return ((px % 2) * 32 + pz * 4 + py, (px // 2) * 2 + pc)

    def shifted(dx, dy, dz, dc):
        return (x + dx) % NX, (y + dy) % NY, (z + dz) % NZ, (c + dc) % NC

    def at(dx=0, dy=0, dz=0, dc=0):
        return device(*shifted(dx, dy, dz, dc))

    far_first = (2, 1, 3)
    near_first = (1, 3, 2)
    sibling = at(dc=1)
    barrier = pltpu.get_barrier_semaphore()
    way = 1 - 2 * c
    following, preceding = at(dz=way + NZ), at(dz=NZ - way)
    crossing = at(dz=way + NZ, dc=1)
    near = [at(dx=d) for d in near_first] + [at(dy=d) for d in near_first] + [sibling, crossing]
    for peer in near + [preceding]:
        pl.semaphore_signal(barrier, inc=1, device_id=peer, device_id_type=MESH)
    load_features = pltpu.make_async_copy(features_hbm, features, load.at[0])
    load_features.start()
    load_start = pltpu.make_async_copy(start_hbm, start_cols.at[c], load.at[1])
    load_start.start()

    load_features.wait()
    values = features[...].astype(F32)
    factor = 1.0 / jnp.sqrt(jnp.sum(values * values, axis=1, keepdims=True) + 1e-06)
    unit = (values * factor).astype(jnp.bfloat16).reshape(2, HALF, -1)
    unit_rows[pl.ds(2 * b, 2)] = unit
    unit_cols[pl.ds(2 * c, 2)] = unit
    pl.semaphore_wait(barrier, len(near) + 1)

    def put(src, dst, stage, arrival, peer):
        pltpu.make_async_remote_copy(
            src_ref=src, dst_ref=dst, send_sem=send.at[stage], recv_sem=arrival,
            device_id=peer, device_id_type=MESH,
        ).start()

    def wait_for(ref, semaphore):
        pltpu.make_async_copy(ref, ref, semaphore).wait()

    def put_row_half(px, py, h, peer, arrival):
        half = unit_rows.at[2 * (px * NY + py) + h]
        put(half, half, UNIT_XY, arrival, peer)

    def slot_of(d, other):
        return (2 * (2 * d - c) if d else 0) + (c + other) % NC

    far_slot = 2 * (NZ - 1) + c

    def hand_on(array, index, ring, d, other, stages, core_arrival):
        stage_z, stage_far, stage_core = stages
        block = array.at[index(slot_of(d, other))]
        if d or other:
            wait_for(block, ring.at[d, other])
        if d < 3:
            put(block, array.at[index(slot_of(d + 1, other))], stage_z, ring.at[d + 1, other], following)
        elif not other:
            for e in range(NC):
                put(block, array.at[index(far_slot)], stage_far, recv.at[stage_far], at(dz=way + NZ, dc=e))
        if not (d or other):
            put(block, block, stage_core, ring.at[0, 1], sibling)
        elif d:
            put(block, block, stage_core, recv.at[core_arrival], sibling)

    def unit_step(d, other):
        for h in range(2):
            hand_on(
                unit_cols, lambda slot: 2 * slot + h, unit_ring.at[h], d, other,
                (UNIT_Z, UNIT_FAR, UNIT_CORE), UNIT_CORE if d < 3 else UNIT_CORE_FAR,
            )

    def start_step(d, other):
        hand_on(
            start_cols, lambda slot: slot, start_ring, d, other, (START_Z, START_FAR, START_CORE), START_CORE
        )

    def plane_step(d):
        px = (x + d) % NX
        wait_for(unit_rows.at[2 * (px * NY + y)], first_hop.at[0, d])
        for e in far_first:
            put_row_half(px, y, 0, at(dy=e), chunk.at[d])
        py = (y + d) % NY
        wait_for(unit_rows.at[2 * (x * NY + py) + 1], first_hop.at[1, d])
        for e in far_first:
            put_row_half(x, py, 1, at(dx=e), chunk.at[NX - e])

    unit_step(0, 0)
    for d in far_first:
        put_row_half(x, y, 0, at(dx=d), first_hop.at[0, NX - d])
        put_row_half(x, y, 1, at(dy=d), first_hop.at[1, NY - d])
    unit_step(0, 1)
    load_start.wait()
    start_step(0, 0)
    for d in range(1, 4):
        unit_step(d, 0)
        if d == 1:
            for e in far_first:
                put_row_half(x, y, 1, at(dx=e), chunk.at[NX - e])
                put_row_half(x, y, 0, at(dy=e), chunk.at[0])
        plane_step((1, 3, 2)[d - 1])
        unit_step(d, 1)
        if d > 1:
            start_step(d - 1, 0)
        start_step(d - 1, 1)

    scale = LOG2E / KERNEL_WIDTH
    side = GROUP * OWN

    def tile_part(d, low, high):
        px = (x + d) % NX
        rows = unit_rows[pl.ds(px * 2 * NY, 2 * NY)].reshape(CHUNK, -1)
        cols = unit_cols[low // HALF : high // HALF].reshape(high - low, -1)
        cosine = lax.dot_general(rows, cols, (((1,), (1,)), ((), ())), preferred_element_type=F32)
        affinity = jnp.exp2(cosine * scale - scale)
        if not (d or low):
            row_id = lax.broadcasted_iota(jnp.int32, (CHUNK, 1), 0) - y * OWN
            row_id = jnp.where((row_id >= 0) & (row_id < OWN), row_id, -2)
            col_id = lax.broadcasted_iota(jnp.int32, (1, high), 1) - c * OWN
            col_id = jnp.where((col_id >= 0) & (col_id < OWN), col_id, -1)
            affinity = jnp.where(row_id == col_id, 0.0, affinity)
        tile[pl.ds(pl.multiple_of(px * CHUNK, CHUNK), CHUNK), low:high] = affinity.astype(jnp.bfloat16)
        return jnp.sum(affinity.reshape(CHUNK // 8, 8, high - low), axis=0)

    def rows_arrived(d):
        wait_for(unit_rows.at[pl.ds(0, 7 if d else 3)], chunk.at[d])

    wait_for(unit_cols.at[pl.ds(0, 8)], recv.at[UNIT_CORE])
    wait_for(unit_cols.at[pl.ds(0, 4)], recv.at[UNIT_CORE_FAR])
    wait_for(unit_cols.at[pl.ds(0, 4)], recv.at[UNIT_FAR])
    near_total = jnp.zeros((8, side), F32)
    for d in (0, 1, 3, 2):
        rows_arrived(d)
        near_total = near_total + tile_part(d, 0, side)
        if not d:
            start_step(3, 0)
            start_step(3, 1)
    for total, low in ((near_total, 0),):
        total = jnp.sum(total, axis=0, keepdims=True)
        for k in range(total.shape[1] // KV):
            pz = (z + COL_ORDER[low // KV + k]) % NZ
            sums[pl.ds(pz, 1), :] = total[:, k * KV : (k + 1) * KV]

    along_z = (4, 5, 3, 6, 2, 7, 1)
    a_peers = [at(dz=d, dc=e) for d in along_z for e in range(NC)] + [sibling]
    b_shifts = [(dx, dy) for dx in (2, 1, 3, 0) for dy in (2, 1, 3, 0) if dx or dy]
    for peer in a_peers:
        put(sums, sums_in.at[a], DEGREES, recv.at[DEGREES], peer)
    sums_in[a] = sums[...]
    wait_for(sums_in.at[pl.ds(0, GROUP - 1)], recv.at[DEGREES])
    inverses[...] = 1.0 / jnp.sqrt(jnp.sum(sums_in[...], axis=0))
    ordered = [inverses[pl.ds((z + r) % NZ, 1), :] for r in COL_ORDER]
    turned = jnp.concatenate(ordered + [jnp.zeros((KV - 8, KV), F32)], axis=0).T
    wait_for(start_cols.at[pl.ds(0, 6)], recv.at[START_CORE])
    wait_for(start_cols.at[pl.ds(0, 2)], recv.at[START_FAR])
    for k in range(8):
        wide = jnp.broadcast_to(turned[:, k : k + 1], (KV, KV))
        inv_cols[k * KV : (k + 1) * KV, :] = wide
        scaled[k * KV : (k + 1) * KV, :] = (
            wide * start_cols[2 * k : 2 * k + 2].reshape(KV, KV)
        ).astype(jnp.bfloat16)
    own_inverse = inv_cols[pl.ds(pl.multiple_of(c * OWN, OWN), OWN), :]

    def image_step(first, d):
        for i, ahead in enumerate((1, NZ - 1)):
            block = image_cols.at[(2 * (2 * d - i) if d else 0) + c]
            if d:
                wait_for(block, image_ring.at[i, d])
            if d < 3:
                put(
                    block, image_cols.at[2 * (2 * d + 2 - i) + c], first + IMAGE_Z, image_ring.at[i, d + 1],
                    at(dz=ahead),
                )
            elif not i:
                for e in range(NC):
                    put(
                        block, image_cols.at[far_slot], first + IMAGE_FAR, recv.at[first + IMAGE_FAR],
                        at(dz=1, dc=e),
                    )
            if d or not i:
                put(block, block, first + IMAGE_CORE, recv.at[first + IMAGE_CORE], sibling)

    for it in range(ITERS):
        first = 9 + 7 * it
        last = it == ITERS - 1
        slots = CHUNK // OWN
        for dx in (2, 1, 3, 0):
            px = (x + dx) % NX
            product = jnp.dot(
                tile[pl.ds(pl.multiple_of(px * CHUNK, CHUNK), CHUNK), :], scaled[...], preferred_element_type=F32
            )
            part[it, pl.ds(px * slots, slots)] = product.reshape(slots, OWN, KV)
            for dy in (2, 1, 3, 0):
                if dx or dy:
                    py = (y + dy) % NY
                    put(
                        part.at[it, px * NY + py], part_in.at[it, b], first + PRODUCT,
                        recv.at[first + PRODUCT], at(dx=dx, dy=dy),
                    )
        part_in[it, b] = part[it, b]
        wait_for(part_in.at[it, pl.ds(0, GROUP - 1)], recv.at[first + PRODUCT])
        image = own_inverse * jnp.sum(part_in[it], axis=0)
        if not last:
            image_cols[c] = image
            image_step(first, 0)
        gram = lax.dot_general(
            image, image, (((0,), (0,)), ((), ())), precision=HIGHEST, preferred_element_type=F32
        )
        gram_part[it] = gram.reshape(GROUP, SLICE, KV)
        for dx, dy in b_shifts:
            px, py, _, _ = shifted(dx, dy, 0, 0)
            put(
                gram_part.at[it, px * NY + py], gram_a.at[it, b], first + GRAM_A,
                recv.at[first + GRAM_A], at(dx=dx, dy=dy),
            )
        gram_a[it, b] = gram_part[it, b]
        if not last:
            image_step(first, 1)
        wait_for(gram_a.at[it, pl.ds(0, GROUP - 1)], recv.at[first + GRAM_A])
        gram_mine[it] = jnp.sum(gram_a[it], axis=0)
        for peer in a_peers:
            put(gram_mine.at[it], gram_b.at[it, a], first + GRAM_B, recv.at[first + GRAM_B], peer)
        gram_b[it, a] = gram_mine[it]
        wait_for(gram_b.at[it, pl.ds(0, GROUP - 1)], recv.at[first + GRAM_B])
        gram_c[it, b] = jnp.sum(gram_b[it], axis=0)
        for dx, dy in b_shifts:
            put(
                gram_c.at[it, b], gram_c.at[it, b], first + GRAM_C, recv.at[first + GRAM_C], at(dx=dx, dy=dy)
            )
        if not last:
            image_step(first, 2)
            image_step(first, 3)
        wait_for(gram_c.at[it, pl.ds(0, GROUP - 1)], recv.at[first + GRAM_C])
        for i, row in enumerate(inverse_cholesky([gram_c[it, i] for i in range(GROUP)])):
            linv[8 * i : 8 * i + 8, :] = row

        def basis(block):
            return lax.dot_general(
                block, linv[...], (((1,), (1,)), ((), ())), precision=HIGHEST, preferred_element_type=F32
            )

        if last:
            vectors = basis(image)
            spread = vectors * jnp.sqrt(F32(NX * NY * NZ * NC * OWN))
            out[...] = vectors / jnp.sqrt(jnp.mean(spread * spread, axis=1, keepdims=True) + 1e-06)
        else:
            wait_for(image_cols.at[pl.ds(0, NZ - 1)], recv.at[first + IMAGE_CORE])
            wait_for(image_cols.at[pl.ds(0, NC)], recv.at[first + IMAGE_FAR])
            for step in range(GROUP * OWN // CHUNK):
                rows = slice(step * CHUNK, (step + 1) * CHUNK)
                vectors = basis(image_cols[step * slots : (step + 1) * slots].reshape(CHUNK, KV))
                scaled[rows, :] = (inv_cols[rows, :] * vectors).astype(jnp.bfloat16)

    for array, halves, stages in (
        (unit_cols, 2, (UNIT_Z, UNIT_FAR, UNIT_CORE)),
        (start_cols, 1, (START_Z, START_FAR, START_CORE)),
    ):
        for stage, blocks in zip(stages, (6, 2, 7)):
            wait_for(array.at[pl.ds(0, blocks * halves)], send.at[stage])
    wait_for(unit_rows.at[pl.ds(0, 30)], send.at[UNIT_XY])
    wait_for(sums_in.at[pl.ds(0, GROUP - 1)], send.at[DEGREES])
    for it in range(ITERS):
        first = 9 + 7 * it
        wait_for(part.at[it, pl.ds(0, GROUP - 1)], send.at[first + PRODUCT])
        for stage in (GRAM_A, GRAM_B, GRAM_C):
            wait_for(gram_a.at[it, pl.ds(0, GROUP - 1)], send.at[first + stage])
        if it < ITERS - 1:
            wait_for(image_cols.at[pl.ds(0, 6)], send.at[first + IMAGE_Z])
            wait_for(image_cols.at[pl.ds(0, 2)], send.at[first + IMAGE_FAR])
            wait_for(image_cols.at[pl.ds(0, 7)], send.at[first + IMAGE_CORE])


def body(features, start):
    own, depth = features.shape
    side = GROUP * OWN
    bf16 = jnp.bfloat16
    hbm = pl.BlockSpec(memory_space=pl.ANY)
    dma = pltpu.SemaphoreType.DMA
    unscaled = pl.pallas_call(
        kernel,
        out_shape=jax.ShapeDtypeStruct((own, KV), F32),
        in_specs=[hbm, hbm],
        out_specs=pl.BlockSpec(memory_space=pltpu.VMEM),
        scratch_shapes=[
            pltpu.VMEM((own, depth), bf16),
            pltpu.VMEM((2 * GROUP, HALF, depth), bf16),
            pltpu.VMEM((2 * GROUP, HALF, depth), bf16),
            pltpu.VMEM((side, side), bf16),
            pltpu.VMEM((GROUP, OWN, KV), F32),
            pltpu.VMEM((8, KV), F32),
            pltpu.VMEM((GROUP, 8, KV), F32),
            pltpu.VMEM((8, KV), F32),
            pltpu.VMEM((side, KV), F32),
            pltpu.VMEM((side, KV), bf16),
            pltpu.VMEM((ITERS, GROUP, OWN, KV), F32),
            pltpu.VMEM((ITERS, GROUP, OWN, KV), F32),
            pltpu.VMEM((GROUP, OWN, KV), F32),
            pltpu.VMEM((ITERS, GROUP, SLICE, KV), F32),
            pltpu.VMEM((ITERS, GROUP, SLICE, KV), F32),
            pltpu.VMEM((ITERS, SLICE, KV), F32),
            pltpu.VMEM((ITERS, GROUP, SLICE, KV), F32),
            pltpu.VMEM((ITERS, GROUP, SLICE, KV), F32),
            pltpu.VMEM((KV, KV), F32),
            dma((2,)),
            dma((STAGES,)),
            dma((STAGES,)),
            dma((2, 4, 2)),
            dma((4, 2)),
            dma((2, 4)),
            dma((2, 4)),
            dma((4,)),
        ],
        compiler_params=pltpu.CompilerParams(
            collective_id=0, has_side_effects=True, vmem_limit_bytes=55200 * 1024
        ),
        name="subspace",
    )(features, start)
    return unscaled * jnp.sqrt(F32(NX * NY * NZ * NC * OWN))


def solution(mesh):
    return jax.shard_map(
        body,
        mesh=mesh,
        in_specs=(P(("blk", "rep"), None), P(("blk", "rep"), None)),
        out_specs=P(("blk", "rep"), None),
        check_vma=False,
    )
```

```python
import functools

import jax
import jax.numpy as jnp
from jax import lax
from jax.experimental import pallas as pl
from jax.experimental.pallas import tpu as pltpu
from jax.sharding import PartitionSpec as P

ITERS = 2
KERNEL_WIDTH = 0.04
LOG2E = 1.4426950408889634
MESH = pl.DeviceIdType.MESH

NX, NY, NZ, NC = 4, 4, 8, 2
GROUP = 16
OWN = 64
KV = 128
SLICE = KV // GROUP
CHUNK = 256
F32 = jnp.float32
HIGHEST = lax.Precision.HIGHEST


def spread_of(v, k, axis):
    return jnp.broadcast_to(v[k : k + 1, :] if axis == 0 else v[:, k : k + 1], v.shape)


PANEL = 2


def inverse_cholesky(rows):
    lane = lax.broadcasted_iota(jnp.int32, (8, KV), 1)
    sub = lax.broadcasted_iota(jnp.int32, (8, KV), 0)
    rows = list(rows)
    width = 8 * PANEL
    out = []
    for p in range(16 // PANEL):
        base = width * p
        own = (lane >= base) & (lane < base + width)
        mine = range(p * PANEL, (p + 1) * PANEL)
        cols = [[spread_of(rows[i], base + k, 1) for i in mine] for k in range(width)]
        panel = [jnp.where(own, (lane - base == sub + 8 * t).astype(F32), rows[i]) for t, i in enumerate(mine)]
        done = [jnp.zeros((8, KV), F32) for _ in mine]
        scale = [jnp.ones((8, KV), F32) for _ in mine]
        for k in range(width):
            t, r = divmod(k, 8)
            pivot = spread_of(cols[k][t], r, 0)
            recip = 1.0 / pivot
            here = sub == r
            others = [jnp.where(here, 0.0, v) if u == t else v for u, v in enumerate(cols[k])]
            for j in range(k + 1, width):
                entry = spread_of(cols[j][t], r, 0)
                cols[j] = [v - (other * entry) * recip for v, other in zip(cols[j], others)]
            done[t] = jnp.where(here, panel[t] * lax.rsqrt(pivot), done[t])
            scale[t] = jnp.where(here, recip, scale[t])
            row = spread_of(panel[t], r, 0)
            panel = [v - (other * row) * recip for v, other in zip(panel, others)]
        panel = [v * factor for v, factor in zip(panel, scale)]
        for t in range(PANEL):
            out.append(jnp.where(lane <= base + 8 * t + sub, done[t], 0.0))
        spreads = [spread_of(panel[k // 8], k % 8, 0) for k in range(width)]
        for i in range((p + 1) * PANEL, 16):
            acc = jnp.where(own, 0.0, rows[i])
            for k in range(width):
                acc = acc - spread_of(rows[i], base + k, 1) * spreads[k]
            rows[i] = acc
    return out


(UNIT_XY, UNIT_Z, UNIT_FAR, UNIT_CORE, UNIT_CORE_FAR, START_Z, START_FAR, START_CORE, DEGREES) = range(9)
(PRODUCT, GRAM_A, GRAM_B, GRAM_C, IMAGE_Z, IMAGE_FAR, IMAGE_CORE) = range(7)
STAGES = 9 + 7 * ITERS
COL_ORDER = (0, 1, 7, 2, 6, 3, 5, 4)
NEAR_COLS = 5 * NC * OWN
HALF = OWN // 2


def kernel(
    features_hbm, start_hbm, out,
    features, unit_rows, unit_cols, tile, start_cols, sums, sums_in, inverses, inv_cols, scaled, part, part_in,
    image_cols, gram_part, gram_a, gram_mine, gram_b, gram_c, linv,
    load, send, recv, unit_ring, start_ring, image_ring, first_hop, chunk,
):
    blk, rep = lax.axis_index("blk"), lax.axis_index("rep")
    x, y, z, c = (rep // 2) * 2 + blk // 32, blk % 4, (blk // 4) % 8, rep % 2
    a, b = c * NZ + z, x * NY + y

    def device(px, py, pz, pc):
        return ((px % 2) * 32 + pz * 4 + py, (px // 2) * 2 + pc)

    def shifted(dx, dy, dz, dc):
        return (x + dx) % NX, (y + dy) % NY, (z + dz) % NZ, (c + dc) % NC

    def at(dx=0, dy=0, dz=0, dc=0):
        return device(*shifted(dx, dy, dz, dc))

    far_first = (2, 1, 3)
    near_first = (1, 3, 2)
    sibling = at(dc=1)
    barrier = pltpu.get_barrier_semaphore()
    way = 1 - 2 * c
    following, preceding = at(dz=way + NZ), at(dz=NZ - way)
    crossing = at(dz=way + NZ, dc=1)
    near = [at(dx=d) for d in near_first] + [at(dy=d) for d in near_first] + [sibling, crossing]
    for peer in near + [preceding]:
        pl.semaphore_signal(barrier, inc=1, device_id=peer, device_id_type=MESH)
    load_features = pltpu.make_async_copy(features_hbm, features, load.at[0])
    load_features.start()
    load_start = pltpu.make_async_copy(start_hbm, start_cols.at[c], load.at[1])
    load_start.start()

    load_features.wait()
    values = features[...].astype(F32)
    factor = 1.0 / jnp.sqrt(jnp.sum(values * values, axis=1, keepdims=True) + 1e-06)
    unit = (values * factor).astype(jnp.bfloat16).reshape(2, HALF, -1)
    unit_rows[pl.ds(2 * b, 2)] = unit
    unit_cols[pl.ds(2 * c, 2)] = unit
    pl.semaphore_wait(barrier, len(near) + 1)

    def put(src, dst, stage, arrival, peer):
        pltpu.make_async_remote_copy(
            src_ref=src, dst_ref=dst, send_sem=send.at[stage], recv_sem=arrival,
            device_id=peer, device_id_type=MESH,
        ).start()

    def wait_for(ref, semaphore):
        pltpu.make_async_copy(ref, ref, semaphore).wait()

    def put_row_half(px, py, h, peer, arrival):
        half = unit_rows.at[2 * (px * NY + py) + h]
        put(half, half, UNIT_XY, arrival, peer)

    def slot_of(d, other):
        return (2 * (2 * d - c) if d else 0) + (c + other) % NC

    far_slot = 2 * (NZ - 1) + c

    def hand_on(array, index, ring, d, other, stages, core_arrival):
        stage_z, stage_far, stage_core = stages
        block = array.at[index(slot_of(d, other))]
        if d or other:
            wait_for(block, ring.at[d, other])
        if d < 3:
            put(block, array.at[index(slot_of(d + 1, other))], stage_z, ring.at[d + 1, other], following)
        elif not other:
            for e in range(NC):
                put(block, array.at[index(far_slot)], stage_far, recv.at[stage_far], at(dz=way + NZ, dc=e))
        if not (d or other):
            put(block, block, stage_core, ring.at[0, 1], sibling)
        elif d:
            put(block, block, stage_core, recv.at[core_arrival], sibling)

    def unit_step(d, other):
        for h in range(2):
            hand_on(
                unit_cols, lambda slot: 2 * slot + h, unit_ring.at[h], d, other,
                (UNIT_Z, UNIT_FAR, UNIT_CORE), UNIT_CORE if d < 3 else UNIT_CORE_FAR,
            )

    def start_step(d, other):
        hand_on(
            start_cols, lambda slot: slot, start_ring, d, other, (START_Z, START_FAR, START_CORE), START_CORE
        )

    def plane_step(d):
        px = (x + d) % NX
        wait_for(unit_rows.at[2 * (px * NY + y)], first_hop.at[0, d])
        for e in far_first:
            put_row_half(px, y, 0, at(dy=e), chunk.at[d])
        py = (y + d) % NY
        wait_for(unit_rows.at[2 * (x * NY + py) + 1], first_hop.at[1, d])
        for e in far_first:
            put_row_half(x, py, 1, at(dx=e), chunk.at[NX - e])

    unit_step(0, 0)
    for d in far_first:
        put_row_half(x, y, 0, at(dx=d), first_hop.at[0, NX - d])
        put_row_half(x, y, 1, at(dy=d), first_hop.at[1, NY - d])
    unit_step(0, 1)
    load_start.wait()
    start_step(0, 0)
    start_step(0, 1)
    for d in range(1, 4):
        unit_step(d, 0)
        if d == 1:
            for e in far_first:
                put_row_half(x, y, 1, at(dx=e), chunk.at[NX - e])
                put_row_half(x, y, 0, at(dy=e), chunk.at[0])
        plane_step((1, 3, 2)[d - 1])
        unit_step(d, 1)
        if d < 3:
            start_step(d, 0)
            start_step(d, 1)

    scale = LOG2E / KERNEL_WIDTH
    side = GROUP * OWN

    def tile_part(d, low, high):
        px = (x + d) % NX
        rows = unit_rows[pl.ds(px * 2 * NY, 2 * NY)].reshape(CHUNK, -1)
        cols = unit_cols[low // HALF : high // HALF].reshape(high - low, -1)
        cosine = lax.dot_general(rows, cols, (((1,), (1,)), ((), ())), preferred_element_type=F32)
        affinity = jnp.exp2(cosine * scale - scale)
        if not (d or low):
            row_id = lax.broadcasted_iota(jnp.int32, (CHUNK, 1), 0) - y * OWN
            row_id = jnp.where((row_id >= 0) & (row_id < OWN), row_id, -2)
            col_id = lax.broadcasted_iota(jnp.int32, (1, high), 1) - c * OWN
            col_id = jnp.where((col_id >= 0) & (col_id < OWN), col_id, -1)
            affinity = jnp.where(row_id == col_id, 0.0, affinity)
        tile[pl.ds(pl.multiple_of(px * CHUNK, CHUNK), CHUNK), low:high] = affinity.astype(jnp.bfloat16)
        return jnp.sum(affinity.reshape(CHUNK // 8, 8, high - low), axis=0)

    def rows_arrived(d):
        wait_for(unit_rows.at[pl.ds(0, 7 if d else 3)], chunk.at[d])

    wait_for(unit_cols.at[pl.ds(0, 8)], recv.at[UNIT_CORE])
    wait_for(unit_cols.at[pl.ds(0, 4)], recv.at[UNIT_CORE_FAR])
    wait_for(unit_cols.at[pl.ds(0, 4)], recv.at[UNIT_FAR])
    near_total = jnp.zeros((8, side), F32)
    for d in (0, 1, 3, 2):
        rows_arrived(d)
        near_total = near_total + tile_part(d, 0, side)
        if not d:
            start_step(3, 0)
            start_step(3, 1)
    for total, low in ((near_total, 0),):
        total = jnp.sum(total, axis=0, keepdims=True)
        for k in range(total.shape[1] // KV):
            pz = (z + COL_ORDER[low // KV + k]) % NZ
            sums[pl.ds(pz, 1), :] = total[:, k * KV : (k + 1) * KV]

    along_z = (4, 5, 3, 6, 2, 7, 1)
    a_peers = [at(dz=d, dc=e) for d in along_z for e in range(NC)] + [sibling]
    b_shifts = [(dx, dy) for dx in (2, 1, 3, 0) for dy in (2, 1, 3, 0) if dx or dy]
    for peer in a_peers:
        put(sums, sums_in.at[a], DEGREES, recv.at[DEGREES], peer)
    sums_in[a] = sums[...]
    for array, pieces, stages in (
        (unit_cols, 2, (UNIT_Z, UNIT_FAR, UNIT_CORE)),
        (start_cols, 1, (START_Z, START_FAR, START_CORE)),
    ):
        for stage, blocks in zip(stages, (6, 2, 7)):
            wait_for(array.at[pl.ds(0, blocks * pieces)], send.at[stage])
    wait_for(unit_rows.at[pl.ds(0, 30)], send.at[UNIT_XY])
    wait_for(sums_in.at[pl.ds(0, GROUP - 1)], send.at[DEGREES])

    def drain_iteration(it):
        first = 9 + 7 * it
        wait_for(part.at[it, pl.ds(0, GROUP - 1)], send.at[first + PRODUCT])
        for stage in (GRAM_A, GRAM_B, GRAM_C):
            wait_for(gram_a.at[it, pl.ds(0, GROUP - 1)], send.at[first + stage])
        if it < ITERS - 1:
            wait_for(image_cols.at[pl.ds(0, 6)], send.at[first + IMAGE_Z])
            wait_for(image_cols.at[pl.ds(0, 2)], send.at[first + IMAGE_FAR])
            wait_for(image_cols.at[pl.ds(0, 7)], send.at[first + IMAGE_CORE])

    wait_for(sums_in.at[pl.ds(0, GROUP - 1)], recv.at[DEGREES])
    inverses[...] = 1.0 / jnp.sqrt(jnp.sum(sums_in[...], axis=0))
    ordered = [inverses[pl.ds((z + r) % NZ, 1), :] for r in COL_ORDER]
    turned = jnp.concatenate(ordered + [jnp.zeros((KV - 8, KV), F32)], axis=0).T
    wait_for(start_cols.at[pl.ds(0, 6)], recv.at[START_CORE])
    wait_for(start_cols.at[pl.ds(0, 2)], recv.at[START_FAR])
    for k in range(8):
        wide = jnp.broadcast_to(turned[:, k : k + 1], (KV, KV))
        inv_cols[k * KV : (k + 1) * KV, :] = wide
        scaled[k * KV : (k + 1) * KV, :] = (
            wide * start_cols[2 * k : 2 * k + 2].reshape(KV, KV)
        ).astype(jnp.bfloat16)
    own_inverse = inv_cols[pl.ds(pl.multiple_of(c * OWN, OWN), OWN), :]

    def image_step(first, d):
        for i, ahead in enumerate((1, NZ - 1)):
            block = image_cols.at[(2 * (2 * d - i) if d else 0) + c]
            if d:
                wait_for(block, image_ring.at[i, d])
            if d < 3:
                put(
                    block, image_cols.at[2 * (2 * d + 2 - i) + c], first + IMAGE_Z, image_ring.at[i, d + 1],
                    at(dz=ahead),
                )
            elif not i:
                for e in range(NC):
                    put(
                        block, image_cols.at[far_slot], first + IMAGE_FAR, recv.at[first + IMAGE_FAR],
                        at(dz=1, dc=e),
                    )
            if d or not i:
                put(block, block, first + IMAGE_CORE, recv.at[first + IMAGE_CORE], sibling)

    for it in range(ITERS):
        first = 9 + 7 * it
        last = it == ITERS - 1
        slots = CHUNK // OWN
        for dx in (2, 1, 3, 0):
            px = (x + dx) % NX
            product = jnp.dot(
                tile[pl.ds(pl.multiple_of(px * CHUNK, CHUNK), CHUNK), :], scaled[...], preferred_element_type=F32
            )
            part[it, pl.ds(px * slots, slots)] = product.reshape(slots, OWN, KV)
            for dy in (2, 1, 3, 0):
                if dx or dy:
                    py = (y + dy) % NY
                    put(
                        part.at[it, px * NY + py], part_in.at[it, b], first + PRODUCT,
                        recv.at[first + PRODUCT], at(dx=dx, dy=dy),
                    )
        part_in[it, b] = part[it, b]
        if it:
            drain_iteration(it - 1)
        wait_for(part_in.at[it, pl.ds(0, GROUP - 1)], recv.at[first + PRODUCT])
        image = own_inverse * jnp.sum(part_in[it], axis=0)
        if not last:
            image_cols[c] = image
            image_step(first, 0)
        gram = lax.dot_general(
            image, image, (((0,), (0,)), ((), ())), precision=HIGHEST, preferred_element_type=F32
        )
        gram_part[it] = gram.reshape(GROUP, SLICE, KV)
        for dx, dy in b_shifts:
            px, py, _, _ = shifted(dx, dy, 0, 0)
            put(
                gram_part.at[it, px * NY + py], gram_a.at[it, b], first + GRAM_A,
                recv.at[first + GRAM_A], at(dx=dx, dy=dy),
            )
        gram_a[it, b] = gram_part[it, b]
        if not last:
            image_step(first, 1)
        wait_for(gram_a.at[it, pl.ds(0, GROUP - 1)], recv.at[first + GRAM_A])
        gram_mine[it] = jnp.sum(gram_a[it], axis=0)
        for peer in a_peers:
            put(gram_mine.at[it], gram_b.at[it, a], first + GRAM_B, recv.at[first + GRAM_B], peer)
        gram_b[it, a] = gram_mine[it]
        wait_for(gram_b.at[it, pl.ds(0, GROUP - 1)], recv.at[first + GRAM_B])
        gram_c[it, b] = jnp.sum(gram_b[it], axis=0)
        for dx, dy in b_shifts:
            put(
                gram_c.at[it, b], gram_c.at[it, b], first + GRAM_C, recv.at[first + GRAM_C], at(dx=dx, dy=dy)
            )
        if not last:
            image_step(first, 2)
            image_step(first, 3)
        wait_for(gram_c.at[it, pl.ds(0, GROUP - 1)], recv.at[first + GRAM_C])
        for i, row in enumerate(inverse_cholesky([gram_c[it, i] for i in range(GROUP)])):
            linv[8 * i : 8 * i + 8, :] = row

        def basis(block):
            return lax.dot_general(
                block, linv[...], (((1,), (1,)), ((), ())), precision=HIGHEST, preferred_element_type=F32
            )

        if last:
            vectors = basis(image)
            spread = vectors * jnp.sqrt(F32(NX * NY * NZ * NC * OWN))
            out[...] = vectors / jnp.sqrt(jnp.mean(spread * spread, axis=1, keepdims=True) + 1e-06)
        else:
            wait_for(image_cols.at[pl.ds(0, NZ - 1)], recv.at[first + IMAGE_CORE])
            wait_for(image_cols.at[pl.ds(0, NC)], recv.at[first + IMAGE_FAR])
            for step in range(GROUP * OWN // CHUNK):
                rows = slice(step * CHUNK, (step + 1) * CHUNK)
                vectors = basis(image_cols[step * slots : (step + 1) * slots].reshape(CHUNK, KV))
                scaled[rows, :] = (inv_cols[rows, :] * vectors).astype(jnp.bfloat16)

    drain_iteration(ITERS - 1)


def body(features, start):
    own, depth = features.shape
    side = GROUP * OWN
    bf16 = jnp.bfloat16
    hbm = pl.BlockSpec(memory_space=pl.ANY)
    dma = pltpu.SemaphoreType.DMA
    unscaled = pl.pallas_call(
        kernel,
        out_shape=jax.ShapeDtypeStruct((own, KV), F32),
        in_specs=[hbm, hbm],
        out_specs=pl.BlockSpec(memory_space=pltpu.VMEM),
        scratch_shapes=[
            pltpu.VMEM((own, depth), bf16),
            pltpu.VMEM((2 * GROUP, HALF, depth), bf16),
            pltpu.VMEM((2 * GROUP, HALF, depth), bf16),
            pltpu.VMEM((side, side), bf16),
            pltpu.VMEM((GROUP, OWN, KV), F32),
            pltpu.VMEM((8, KV), F32),
            pltpu.VMEM((GROUP, 8, KV), F32),
            pltpu.VMEM((8, KV), F32),
            pltpu.VMEM((side, KV), F32),
            pltpu.VMEM((side, KV), bf16),
            pltpu.VMEM((ITERS, GROUP, OWN, KV), F32),
            pltpu.VMEM((ITERS, GROUP, OWN, KV), F32),
            pltpu.VMEM((GROUP, OWN, KV), F32),
            pltpu.VMEM((ITERS, GROUP, SLICE, KV), F32),
            pltpu.VMEM((ITERS, GROUP, SLICE, KV), F32),
            pltpu.VMEM((ITERS, SLICE, KV), F32),
            pltpu.VMEM((ITERS, GROUP, SLICE, KV), F32),
            pltpu.VMEM((ITERS, GROUP, SLICE, KV), F32),
            pltpu.VMEM((KV, KV), F32),
            dma((2,)),
            dma((STAGES,)),
            dma((STAGES,)),
            dma((2, 4, 2)),
            dma((4, 2)),
            dma((2, 4)),
            dma((2, 4)),
            dma((4,)),
        ],
        compiler_params=pltpu.CompilerParams(
            collective_id=0, has_side_effects=True, vmem_limit_bytes=55200 * 1024
        ),
        name="subspace",
    )(features, start)
    return unscaled * jnp.sqrt(F32(NX * NY * NZ * NC * OWN))


def solution(mesh):
    return jax.shard_map(
        body,
        mesh=mesh,
        in_specs=(P(("blk", "rep"), None), P(("blk", "rep"), None)),
        out_specs=P(("blk", "rep"), None),
        check_vma=False,
    )
```

```python
import functools

import jax
import jax.numpy as jnp
from jax import lax
from jax.experimental import pallas as pl
from jax.experimental.pallas import tpu as pltpu
from jax.sharding import PartitionSpec as P

ITERS = 2
KERNEL_WIDTH = 0.04
LOG2E = 1.4426950408889634
MESH = pl.DeviceIdType.MESH

NX, NY, NZ, NC = 4, 4, 8, 2
GROUP = 16
OWN = 64
KV = 128
SLICE = KV // GROUP
CHUNK = 256
F32 = jnp.float32
HIGHEST = lax.Precision.HIGHEST


def spread_of(v, k, axis):
    return jnp.broadcast_to(v[k : k + 1, :] if axis == 0 else v[:, k : k + 1], v.shape)


PANEL = 2


def inverse_cholesky(rows):
    lane = lax.broadcasted_iota(jnp.int32, (8, KV), 1)
    sub = lax.broadcasted_iota(jnp.int32, (8, KV), 0)
    rows = list(rows)
    width = 8 * PANEL
    out = []
    for p in range(16 // PANEL):
        base = width * p
        own = (lane >= base) & (lane < base + width)
        mine = range(p * PANEL, (p + 1) * PANEL)
        cols = [[spread_of(rows[i], base + k, 1) for i in mine] for k in range(width)]
        panel = [jnp.where(own, (lane - base == sub + 8 * t).astype(F32), rows[i]) for t, i in enumerate(mine)]
        done = [jnp.zeros((8, KV), F32) for _ in mine]
        scale = [jnp.ones((8, KV), F32) for _ in mine]
        for k in range(width):
            t, r = divmod(k, 8)
            if k % 4 == 0:
                block = {
                    (j, m): spread_of(cols[m][t], j % 8, 0) for m in range(k, k + 4) for j in range(m, k + 4)
                }
                recips = {}
                for q in range(k, k + 4):
                    recips[q] = 1.0 / block[q, q]
                    for m in range(q + 1, k + 4):
                        for j in range(m, k + 4):
                            block[j, m] = block[j, m] - (block[j, q] * block[m, q]) * recips[q]
            pivot, recip = block[k, k], recips[k]
            here = sub == r
            others = [jnp.where(here, 0.0, v) if u == t else v for u, v in enumerate(cols[k])]
            for j in range(k + 1, width):
                entry = spread_of(cols[j][t], r, 0)
                cols[j] = [v - (other * entry) * recip for v, other in zip(cols[j], others)]
            done[t] = jnp.where(here, panel[t] * lax.rsqrt(pivot), done[t])
            scale[t] = jnp.where(here, recip, scale[t])
            row = spread_of(panel[t], r, 0)
            panel = [v - (other * row) * recip for v, other in zip(panel, others)]
        panel = [v * factor for v, factor in zip(panel, scale)]
        for t in range(PANEL):
            out.append(jnp.where(lane <= base + 8 * t + sub, done[t], 0.0))
        spreads = [spread_of(panel[k // 8], k % 8, 0) for k in range(width)]
        for i in range((p + 1) * PANEL, 16):
            acc = jnp.where(own, 0.0, rows[i])
            for k in range(width):
                acc = acc - spread_of(rows[i], base + k, 1) * spreads[k]
            rows[i] = acc
    return out


(UNIT_XY, UNIT_Z, UNIT_FAR, UNIT_CORE, UNIT_CORE_FAR, START_Z, START_FAR, START_CORE, DEGREES) = range(9)
(PRODUCT, GRAM_A, GRAM_B, GRAM_C, IMAGE_Z, IMAGE_FAR, IMAGE_CORE) = range(7)
STAGES = 9 + 7 * ITERS
COL_ORDER = (0, 1, 7, 2, 6, 3, 5, 4)
NEAR_COLS = 5 * NC * OWN
HALF = OWN // 2
PIECES = 4
PIECE = OWN // PIECES


def kernel(
    features_hbm, start_hbm, out,
    features, unit_rows, unit_cols, tile, start_cols, sums, sums_in, inverses, inv_cols, scaled, part, part_in,
    image_cols, gram_part, gram_a, gram_mine, gram_b, gram_c, linv,
    load, send, recv, unit_ring, start_ring, image_ring, first_hop, chunk,
):
    blk, rep = lax.axis_index("blk"), lax.axis_index("rep")
    x, y, z, c = (rep // 2) * 2 + blk // 32, blk % 4, (blk // 4) % 8, rep % 2
    a, b = c * NZ + z, x * NY + y

    def device(px, py, pz, pc):
        return ((px % 2) * 32 + pz * 4 + py, (px // 2) * 2 + pc)

    def shifted(dx, dy, dz, dc):
        return (x + dx) % NX, (y + dy) % NY, (z + dz) % NZ, (c + dc) % NC

    def at(dx=0, dy=0, dz=0, dc=0):
        return device(*shifted(dx, dy, dz, dc))

    far_first = (2, 1, 3)
    near_first = (1, 3, 2)
    sibling = at(dc=1)
    barrier = pltpu.get_barrier_semaphore()
    way = 1 - 2 * c
    following, preceding = at(dz=way + NZ), at(dz=NZ - way)
    crossing = at(dz=way + NZ, dc=1)
    near = [at(dx=d) for d in near_first] + [at(dy=d) for d in near_first] + [sibling, crossing]
    for peer in near + [preceding]:
        pl.semaphore_signal(barrier, inc=1, device_id=peer, device_id_type=MESH)
    load_features = pltpu.make_async_copy(features_hbm, features, load.at[0])
    load_features.start()
    load_start = pltpu.make_async_copy(start_hbm, start_cols.at[c], load.at[1])
    load_start.start()

    load_features.wait()
    values = features[...].astype(F32)
    factor = 1.0 / jnp.sqrt(jnp.sum(values * values, axis=1, keepdims=True) + 1e-06)
    unit = (values * factor).astype(jnp.bfloat16)
    unit_rows[pl.ds(2 * b, 2)] = unit.reshape(2, HALF, -1)
    unit_cols[pl.ds(PIECES * c, PIECES)] = unit.reshape(PIECES, PIECE, -1)
    pl.semaphore_wait(barrier, len(near) + 1)

    def put(src, dst, stage, arrival, peer):
        pltpu.make_async_remote_copy(
            src_ref=src, dst_ref=dst, send_sem=send.at[stage], recv_sem=arrival,
            device_id=peer, device_id_type=MESH,
        ).start()

    def wait_for(ref, semaphore):
        pltpu.make_async_copy(ref, ref, semaphore).wait()

    def put_row_half(px, py, h, peer, arrival):
        half = unit_rows.at[2 * (px * NY + py) + h]
        put(half, half, UNIT_XY, arrival, peer)

    def slot_of(d, other):
        return (2 * (2 * d - c) if d else 0) + (c + other) % NC

    far_slot = 2 * (NZ - 1) + c

    def hand_on(array, index, ring, d, other, stages, core_arrival):
        stage_z, stage_far, stage_core = stages
        block = array.at[index(slot_of(d, other))]
        if d or other:
            wait_for(block, ring.at[d, other])
        if d < 3:
            put(block, array.at[index(slot_of(d + 1, other))], stage_z, ring.at[d + 1, other], following)
        elif not other:
            for e in range(NC):
                put(block, array.at[index(far_slot)], stage_far, recv.at[stage_far], at(dz=way + NZ, dc=e))
        if not (d or other):
            put(block, block, stage_core, ring.at[0, 1], sibling)
        elif d:
            put(block, block, stage_core, recv.at[core_arrival], sibling)

    def unit_step(d, other):
        for h in range(PIECES):
            hand_on(
                unit_cols, lambda slot: PIECES * slot + h, unit_ring.at[h], d, other,
                (UNIT_Z, UNIT_FAR, UNIT_CORE), UNIT_CORE if d < 3 else UNIT_CORE_FAR,
            )

    def start_step(d, other):
        hand_on(
            start_cols, lambda slot: slot, start_ring, d, other, (START_Z, START_FAR, START_CORE), START_CORE
        )

    def plane_step(d):
        px = (x + d) % NX
        wait_for(unit_rows.at[2 * (px * NY + y)], first_hop.at[0, d])
        for e in far_first:
            put_row_half(px, y, 0, at(dy=e), chunk.at[d])
        py = (y + d) % NY
        wait_for(unit_rows.at[2 * (x * NY + py) + 1], first_hop.at[1, d])
        for e in far_first:
            put_row_half(x, py, 1, at(dx=e), chunk.at[NX - e])

    unit_step(0, 0)
    for d in far_first:
        put_row_half(x, y, 0, at(dx=d), first_hop.at[0, NX - d])
        put_row_half(x, y, 1, at(dy=d), first_hop.at[1, NY - d])
    unit_step(0, 1)
    load_start.wait()
    start_step(0, 0)
    start_step(0, 1)
    for d in range(1, 4):
        unit_step(d, 0)
        if d == 1:
            for e in far_first:
                put_row_half(x, y, 1, at(dx=e), chunk.at[NX - e])
                put_row_half(x, y, 0, at(dy=e), chunk.at[0])
        plane_step((1, 3, 2)[d - 1])
        unit_step(d, 1)
        if d < 3:
            start_step(d, 0)
            start_step(d, 1)

    scale = LOG2E / KERNEL_WIDTH
    side = GROUP * OWN

    def tile_part(d, low, high):
        px = (x + d) % NX
        rows = unit_rows[pl.ds(px * 2 * NY, 2 * NY)].reshape(CHUNK, -1)
        cols = unit_cols[low // PIECE : high // PIECE].reshape(high - low, -1)
        cosine = lax.dot_general(rows, cols, (((1,), (1,)), ((), ())), preferred_element_type=F32)
        affinity = jnp.exp2(cosine * scale - scale)
        if not (d or low):
            row_id = lax.broadcasted_iota(jnp.int32, (CHUNK, 1), 0) - y * OWN
            row_id = jnp.where((row_id >= 0) & (row_id < OWN), row_id, -2)
            col_id = lax.broadcasted_iota(jnp.int32, (1, high), 1) - c * OWN
            col_id = jnp.where((col_id >= 0) & (col_id < OWN), col_id, -1)
            affinity = jnp.where(row_id == col_id, 0.0, affinity)
        tile[pl.ds(pl.multiple_of(px * CHUNK, CHUNK), CHUNK), low:high] = affinity.astype(jnp.bfloat16)
        return jnp.sum(affinity.reshape(CHUNK // 8, 8, high - low), axis=0)

    def rows_arrived(d):
        wait_for(unit_rows.at[pl.ds(0, 7 if d else 3)], chunk.at[d])

    wait_for(unit_cols.at[pl.ds(0, 4 * PIECES)], recv.at[UNIT_CORE])
    wait_for(unit_cols.at[pl.ds(0, 2 * PIECES)], recv.at[UNIT_CORE_FAR])
    wait_for(unit_cols.at[pl.ds(0, 2 * PIECES)], recv.at[UNIT_FAR])
    near_total = jnp.zeros((8, side), F32)
    for d in (0, 1, 3, 2):
        rows_arrived(d)
        near_total = near_total + tile_part(d, 0, side)
        if not d:
            start_step(3, 0)
            start_step(3, 1)
    for total, low in ((near_total, 0),):
        total = jnp.sum(total, axis=0, keepdims=True)
        for k in range(total.shape[1] // KV):
            pz = (z + COL_ORDER[low // KV + k]) % NZ
            sums[pl.ds(pz, 1), :] = total[:, k * KV : (k + 1) * KV]

    along_z = (4, 5, 3, 6, 2, 7, 1)
    a_peers = [at(dz=d, dc=e) for d in along_z for e in range(NC)] + [sibling]
    b_shifts = [(dx, dy) for dx in (2, 1, 3, 0) for dy in (2, 1, 3, 0) if dx or dy]
    for peer in a_peers:
        put(sums, sums_in.at[a], DEGREES, recv.at[DEGREES], peer)
    sums_in[a] = sums[...]
    for array, pieces, stages in (
        (unit_cols, PIECES, (UNIT_Z, UNIT_FAR, UNIT_CORE)),
        (start_cols, 1, (START_Z, START_FAR, START_CORE)),
    ):
        for stage, blocks in zip(stages, (6, 2, 7)):
            wait_for(array.at[pl.ds(0, blocks * pieces)], send.at[stage])
    wait_for(unit_rows.at[pl.ds(0, 30)], send.at[UNIT_XY])
    wait_for(sums_in.at[pl.ds(0, GROUP - 1)], send.at[DEGREES])

    def drain_iteration(it):
        first = 9 + 7 * it
        wait_for(part.at[it, pl.ds(0, GROUP - 1)], send.at[first + PRODUCT])
        for stage in (GRAM_A, GRAM_B, GRAM_C):
            wait_for(gram_a.at[it, pl.ds(0, GROUP - 1)], send.at[first + stage])
        if it < ITERS - 1:
            wait_for(image_cols.at[pl.ds(0, 6)], send.at[first + IMAGE_Z])
            wait_for(image_cols.at[pl.ds(0, 2)], send.at[first + IMAGE_FAR])
            wait_for(image_cols.at[pl.ds(0, 7)], send.at[first + IMAGE_CORE])

    wait_for(sums_in.at[pl.ds(0, GROUP - 1)], recv.at[DEGREES])
    inverses[...] = 1.0 / jnp.sqrt(jnp.sum(sums_in[...], axis=0))
    ordered = [inverses[pl.ds((z + r) % NZ, 1), :] for r in COL_ORDER]
    turned = jnp.concatenate(ordered + [jnp.zeros((KV - 8, KV), F32)], axis=0).T
    wait_for(start_cols.at[pl.ds(0, 6)], recv.at[START_CORE])
    wait_for(start_cols.at[pl.ds(0, 2)], recv.at[START_FAR])
    for k in range(8):
        wide = jnp.broadcast_to(turned[:, k : k + 1], (KV, KV))
        inv_cols[k * KV : (k + 1) * KV, :] = wide
        scaled[k * KV : (k + 1) * KV, :] = (
            wide * start_cols[2 * k : 2 * k + 2].reshape(KV, KV)
        ).astype(jnp.bfloat16)
    own_inverse = inv_cols[pl.ds(pl.multiple_of(c * OWN, OWN), OWN), :]

    def image_step(first, d):
        for i, ahead in enumerate((1, NZ - 1)):
            block = image_cols.at[(2 * (2 * d - i) if d else 0) + c]
            if d:
                wait_for(block, image_ring.at[i, d])
            if d < 3:
                put(
                    block, image_cols.at[2 * (2 * d + 2 - i) + c], first + IMAGE_Z, image_ring.at[i, d + 1],
                    at(dz=ahead),
                )
            elif not i:
                for e in range(NC):
                    put(
                        block, image_cols.at[far_slot], first + IMAGE_FAR, recv.at[first + IMAGE_FAR],
                        at(dz=1, dc=e),
                    )
            if d or not i:
                put(block, block, first + IMAGE_CORE, recv.at[first + IMAGE_CORE], sibling)

    for it in range(ITERS):
        first = 9 + 7 * it
        last = it == ITERS - 1
        slots = CHUNK // OWN
        for dx in (2, 1, 3, 0):
            px = (x + dx) % NX
            product = jnp.dot(
                tile[pl.ds(pl.multiple_of(px * CHUNK, CHUNK), CHUNK), :], scaled[...], preferred_element_type=F32
            )
            part[it, pl.ds(px * slots, slots)] = product.reshape(slots, OWN, KV)
            for dy in (2, 1, 3, 0):
                if dx or dy:
                    py = (y + dy) % NY
                    put(
                        part.at[it, px * NY + py], part_in.at[it, b], first + PRODUCT,
                        recv.at[first + PRODUCT], at(dx=dx, dy=dy),
                    )
        part_in[it, b] = part[it, b]
        if it:
            drain_iteration(it - 1)
        wait_for(part_in.at[it, pl.ds(0, GROUP - 1)], recv.at[first + PRODUCT])
        image = own_inverse * jnp.sum(part_in[it], axis=0)
        if not last:
            image_cols[c] = image
            image_step(first, 0)
        gram = lax.dot_general(
            image, image, (((0,), (0,)), ((), ())), precision=HIGHEST, preferred_element_type=F32
        )
        gram_part[it] = gram.reshape(GROUP, SLICE, KV)
        for dx, dy in b_shifts:
            px, py, _, _ = shifted(dx, dy, 0, 0)
            put(
                gram_part.at[it, px * NY + py], gram_a.at[it, b], first + GRAM_A,
                recv.at[first + GRAM_A], at(dx=dx, dy=dy),
            )
        gram_a[it, b] = gram_part[it, b]
        if not last:
            image_step(first, 1)
        wait_for(gram_a.at[it, pl.ds(0, GROUP - 1)], recv.at[first + GRAM_A])
        gram_mine[it] = jnp.sum(gram_a[it], axis=0)
        for peer in a_peers:
            put(gram_mine.at[it], gram_b.at[it, a], first + GRAM_B, recv.at[first + GRAM_B], peer)
        gram_b[it, a] = gram_mine[it]
        wait_for(gram_b.at[it, pl.ds(0, GROUP - 1)], recv.at[first + GRAM_B])
        gram_c[it, b] = jnp.sum(gram_b[it], axis=0)
        for dx, dy in b_shifts:
            put(
                gram_c.at[it, b], gram_c.at[it, b], first + GRAM_C, recv.at[first + GRAM_C], at(dx=dx, dy=dy)
            )
        if not last:
            image_step(first, 2)
            image_step(first, 3)
        wait_for(gram_c.at[it, pl.ds(0, GROUP - 1)], recv.at[first + GRAM_C])
        for i, row in enumerate(inverse_cholesky([gram_c[it, i] for i in range(GROUP)])):
            linv[8 * i : 8 * i + 8, :] = row

        def basis(block):
            return lax.dot_general(
                block, linv[...], (((1,), (1,)), ((), ())), precision=HIGHEST, preferred_element_type=F32
            )

        if last:
            vectors = basis(image)
            spread = vectors * jnp.sqrt(F32(NX * NY * NZ * NC * OWN))
            out[...] = vectors / jnp.sqrt(jnp.mean(spread * spread, axis=1, keepdims=True) + 1e-06)
        else:
            wait_for(image_cols.at[pl.ds(0, NZ - 1)], recv.at[first + IMAGE_CORE])
            wait_for(image_cols.at[pl.ds(0, NC)], recv.at[first + IMAGE_FAR])
            for step in range(GROUP * OWN // CHUNK):
                rows = slice(step * CHUNK, (step + 1) * CHUNK)
                vectors = basis(image_cols[step * slots : (step + 1) * slots].reshape(CHUNK, KV))
                scaled[rows, :] = (inv_cols[rows, :] * vectors).astype(jnp.bfloat16)

    drain_iteration(ITERS - 1)


def body(features, start):
    own, depth = features.shape
    side = GROUP * OWN
    bf16 = jnp.bfloat16
    hbm = pl.BlockSpec(memory_space=pl.ANY)
    dma = pltpu.SemaphoreType.DMA
    unscaled = pl.pallas_call(
        kernel,
        out_shape=jax.ShapeDtypeStruct((own, KV), F32),
        in_specs=[hbm, hbm],
        out_specs=pl.BlockSpec(memory_space=pltpu.VMEM),
        scratch_shapes=[
            pltpu.VMEM((own, depth), bf16),
            pltpu.VMEM((2 * GROUP, HALF, depth), bf16),
            pltpu.VMEM((PIECES * GROUP, PIECE, depth), bf16),
            pltpu.VMEM((side, side), bf16),
            pltpu.VMEM((GROUP, OWN, KV), F32),
            pltpu.VMEM((8, KV), F32),
            pltpu.VMEM((GROUP, 8, KV), F32),
            pltpu.VMEM((8, KV), F32),
            pltpu.VMEM((side, KV), F32),
            pltpu.VMEM((side, KV), bf16),
            pltpu.VMEM((ITERS, GROUP, OWN, KV), F32),
            pltpu.VMEM((ITERS, GROUP, OWN, KV), F32),
            pltpu.VMEM((GROUP, OWN, KV), F32),
            pltpu.VMEM((ITERS, GROUP, SLICE, KV), F32),
            pltpu.VMEM((ITERS, GROUP, SLICE, KV), F32),
            pltpu.VMEM((ITERS, SLICE, KV), F32),
            pltpu.VMEM((ITERS, GROUP, SLICE, KV), F32),
            pltpu.VMEM((ITERS, GROUP, SLICE, KV), F32),
            pltpu.VMEM((KV, KV), F32),
            dma((2,)),
            dma((STAGES,)),
            dma((STAGES,)),
            dma((PIECES, 4, 2)),
            dma((4, 2)),
            dma((2, 4)),
            dma((2, 4)),
            dma((4,)),
        ],
        compiler_params=pltpu.CompilerParams(
            collective_id=0, has_side_effects=True, vmem_limit_bytes=55200 * 1024
        ),
        name="subspace",
    )(features, start)
    return unscaled * jnp.sqrt(F32(NX * NY * NZ * NC * OWN))


def solution(mesh):
    return jax.shard_map(
        body,
        mesh=mesh,
        in_specs=(P(("blk", "rep"), None), P(("blk", "rep"), None)),
        out_specs=P(("blk", "rep"), None),
        check_vma=False,
    )
```
